128 devices in a mesh: seq: 16 (over x, y), ep: 8 (over z, core).
Axes of the slice: x: 4, y: 4, z: 4, core: 2. Of those that a mesh axis runs over, the one named last changes fastest.
Arguments:
- latent_cache: bfloat16 [128, 16384, 576], P('ep', 'seq'), may hold values from -6 to 6
- queries: bfloat16 [128, 128, 576], P('ep', 'seq'), may hold values from -12 to 12
- lengths: int32 [128], P('ep'), may hold values from 2 to 16384, as said below
- up_value: bfloat16 [128, 512, 128], P(('seq', 'ep')), may hold values from -1.1953125 to 1.1953125
- out_proj: bfloat16 [128, 128, 7168], P(('seq', 'ep')), may hold values from -0.1875 to 0.1875
- residual: bfloat16 [128, 7168], P(('seq', 'ep')), may hold values from -10 to 10
- norm_gain: bfloat16 [7168], replicated, may hold values from 0.099609375 to 1.8984375
- routes: int32 [128, 8], P(('seq', 'ep')), may hold values from 0 to 15, all different within a row
- route_weight: float32 [128, 8], P(('seq', 'ep')), may hold values from 0.1 to 1
- expert_gate: bfloat16 [16, 7168, 1024], P('seq', None, 'ep'), may hold values from -0.0625 to 0.0625
- expert_up: bfloat16 [16, 7168, 1024], P('seq', None, 'ep'), may hold values from -0.0625 to 0.0625
- expert_down: bfloat16 [16, 1024, 7168], P('seq', 'ep'), may hold values from -0.1875 to 0.1875
Outputs:
- mixed: bfloat16 [128, 7168], P(('seq', 'ep'))
The draws below stay inside these ranges and needn't reach their ends.
Inputs may be any that keep to these rules, and one draw needn't show every extreme that they name: `lengths`: some sequence uses all 16384 positions. `routes`: each row names 8 different experts.
All inputs are finite; a program needn't handle non-finite values.
Results may differ from the reference program's by a relative error of at most 0.035.
Values may be sent and summed in bfloat16 or wider, within the bound.
A program may use at most 128 MiB of HBM per device.

```python
import math
import jax
import jax.numpy as jnp
from jax import lax

D = 7168
LAT = 512
VDIM = 128
HEADS = 128
FFE = 1024
EXPERTS = 16
TOPK = 8
SEQS = 128
CONTEXT = 16384
BLK = 512
KDIM = 576


def aligned_rows(key):
    key = jax.random.fold_in(key, 101)
    subkeys = jax.random.split(key, 6)
    lengths = jax.random.randint(subkeys[0], (SEQS,), 2, CONTEXT + 1, dtype=jnp.int32)
    longest = jax.random.randint(subkeys[1], (), 0, SEQS, dtype=jnp.int32)
    lengths = lengths.at[longest].set(CONTEXT)
    chosen = jax.random.permutation(subkeys[2], SEQS)[:3].astype(jnp.int32)
    head_rows = jax.random.randint(subkeys[3], (3,), 0, HEADS, dtype=jnp.int32)
    sign_rows = 2.0 * jax.random.bernoulli(subkeys[4], 0.5, (3, KDIM)).astype(jnp.float32) - 1.0
    others = 2.0 * jax.random.bernoulli(subkeys[5], 0.5, (3, KDIM)).astype(jnp.float32) - 1.0
    return (lengths, chosen, head_rows, sign_rows, others)


def draw_lengths(key, part):
    shared = aligned_rows(key)
    return shared[0]


def draw_queries(key, part):
    key = jax.random.fold_in(key, 2)
    drawn = jnp.clip(1.2 * jax.random.normal(key, (SEQS, HEADS, KDIM), jnp.float32), -7.2, 7.2)
    return drawn.astype(jnp.bfloat16)


def draw_latent_cache(key, part):
    key = jax.random.fold_in(key, 3)
    full_shape = (SEQS, CONTEXT, KDIM)
    drawn = jnp.clip(jax.random.normal(key, full_shape, jnp.float32), -6.0, 6.0)
    return drawn.astype(jnp.bfloat16)


def draw_residual(key, part):
    key = jax.random.fold_in(key, 4)
    subkeys = jax.random.split(key, 4)
    col_scale = jnp.exp(jax.random.uniform(subkeys[1], (1, D), jnp.float32, math.log(0.2), math.log(2.0)))
    row_scale = jnp.exp(jax.random.uniform(subkeys[0], (SEQS, 1), jnp.float32, math.log(0.6), math.log(1.6)))
    noise = jnp.clip(jax.random.normal(subkeys[3], (SEQS, D), jnp.float32), -3.0, 3.0)
    drawn = noise * row_scale * col_scale
    return drawn.astype(jnp.bfloat16)


def raised(values, rng, source, target, shards_of, factor):
    def block_of(position):
        return (jnp.arange(values.shape[position]) // (values.shape[position] // shards_of)).reshape((-1,) + (1,) * (values.ndim - 1 - position))

    one_side = jax.random.permutation(rng, shards_of)[block_of(target)]
    other_side = (block_of(target) + shards_of // 2) % shards_of
    return jnp.where((block_of(source) == one_side) | (block_of(source) == other_side), factor * values, values)


def levels(key, shape, shards, low, top_value):
    def one(dim, parts):
        heights = jax.random.uniform(jax.random.fold_in(jax.random.fold_in(key, 6), dim), (parts,), jnp.float32, low / len(shards), top_value / len(shards))
        return jnp.repeat(jnp.exp(heights), shape[dim] // parts).reshape((-1,) + (1,) * (len(shape) - dim - 1))

    factor_of = one(*shards[0])
    for cut in shards[1:]:
        factor_of = factor_of * one(*cut)
    return factor_of


def picks_of(own_key, rows, count, top, lift):
    order = jax.random.permutation(jax.random.fold_in(own_key, 1), count)
    favour = order
    for power in range(3):
        favour = favour * favour // count
    favour = favour * lift // count
    tickets = jax.random.randint(jax.random.fold_in(own_key, 2), (rows, count), 0, 4096) + favour
    fixed_rows = jax.random.permutation(jax.random.fold_in(own_key, 3), rows)[jnp.arange(count) % rows]
    tickets = jnp.where(jnp.arange(rows)[:, None] == fixed_rows[None, :], 1 << 14, tickets)
    priority = tickets * count + jnp.arange(count)
    return lax.top_k(priority.astype(jnp.int32), top)[1].astype(jnp.int32)


def bell_draw(own_key, dims, deviation, limit, cuts=(), held_as=jnp.bfloat16):
    entries = deviation * jax.random.normal(own_key, dims, jnp.float32)
    if cuts:
        entries = entries * levels(own_key, dims, cuts, -0.22, 0.18)
    return jnp.clip(entries, -limit, limit).astype(held_as)


def gaussian_with(stream_key, extent, spread, most, cuts, heavy, kind=jnp.bfloat16):
    values = spread * jax.random.normal(stream_key, extent, jnp.float32)
    if cuts:
        values = values * levels(stream_key, extent, cuts, -0.22, 0.18)
    return jnp.clip(raised(values, jax.random.fold_in(stream_key, 3), *heavy), -most, most).astype(kind)


def setup_inputs(seed: int = 0) -> dict:
    streams_of = jax.random.split(jax.random.key(seed), 13)
    latent_cache = draw_latent_cache(jax.random.fold_in(streams_of[12], 71), 0)
    queries = draw_queries(jax.random.fold_in(streams_of[12], 71), 0)
    lengths = draw_lengths(jax.random.fold_in(streams_of[12], 71), 0)
    up_value = bell_draw(streams_of[3], (HEADS, LAT, VDIM), 0.2, 1.1953125, ((0, 128),))
    out_proj = gaussian_with(streams_of[4], (HEADS, VDIM, D), (HEADS * VDIM) ** -0.5, 0.1875, ((0, 128),), (0, 2, 128, 5.5))
    residual = draw_residual(jax.random.fold_in(streams_of[12], 71), 0)
    norm_gain = jnp.clip(1.0 + 0.18 * jax.random.normal(streams_of[6], (D,), jnp.float32), 0.099609375, 1.8984375).astype(jnp.bfloat16)
    routes = picks_of(streams_of[7], SEQS, EXPERTS, TOPK, 8192)
    route_weight = jnp.clip(0.1 + 0.9 * jax.random.uniform(streams_of[8], (SEQS, TOPK), jnp.float32) ** levels(streams_of[8], (SEQS, TOPK), ((0, 128),), -0.2, 0.2), 0.1, 1.0)
    expert_gate = bell_draw(streams_of[9], (EXPERTS, D, FFE), D ** -0.5, 0.0625, ((0, 16), (2, 8)))
    expert_up = bell_draw(streams_of[10], (EXPERTS, D, FFE), D ** -0.5, 0.0625, ((0, 16), (2, 8)))
    expert_down = bell_draw(streams_of[11], (EXPERTS, FFE, D), FFE ** -0.5, 0.1875, ((0, 16), (1, 8)))
    return {"latent_cache": latent_cache, "queries": queries, "lengths": lengths, "up_value": up_value, "out_proj": out_proj, "residual": residual, "norm_gain": norm_gain, "routes": routes, "route_weight": route_weight, "expert_gate": expert_gate, "expert_up": expert_up, "expert_down": expert_down}


score_scale = 192.0 ** (-0.5)
masked_score = -1e+30

def attend_sequence(inputs):
    query_row, cache_rows, length = inputs
    query_wide = query_row.astype(jnp.float32)

    def one_block(carry, block_index):
        row_top, row_total, summed = carry
        block_start = block_index * BLK
        key_block = lax.dynamic_slice_in_dim(cache_rows, block_start, BLK, 0).astype(jnp.float32)
        scores = jnp.einsum('hk,tk->ht', query_wide, key_block) * score_scale
        is_live = block_start + jnp.arange(BLK, dtype=jnp.int32) < length
        scores = jnp.where(is_live[None, :], scores, masked_score)
        block_top = lax.optimization_barrier(jnp.max(scores, axis=1))
        exp_scores = jnp.where(is_live[None, :], jnp.exp(scores - block_top[:, None]), 0.0)
        block_total = lax.optimization_barrier(jnp.sum(exp_scores, axis=1))
        rounded = lax.optimization_barrier(exp_scores.astype(jnp.bfloat16)).astype(jnp.float32)
        block_sum = jnp.einsum('ht,tl->hl', rounded, key_block[:, :LAT])
        new_top = jnp.maximum(row_top, block_top)
        old_weight = jnp.exp(row_top - new_top)
        new_weight = jnp.exp(block_top - new_top)
        row_total = row_total * old_weight + block_total * new_weight
        summed = summed * old_weight[:, None] + block_sum * new_weight[:, None]
        return ((new_top, row_total, summed), None)
    initial = (jnp.full((HEADS,), masked_score, jnp.float32), jnp.zeros((HEADS,), jnp.float32), jnp.zeros((HEADS, LAT), jnp.float32))
    finals, _ = lax.scan(one_block, initial, jnp.arange(CONTEXT // BLK, dtype=jnp.int32))
    return (finals[2] / finals[1][:, None]).astype(jnp.bfloat16)

def reference(latent_cache, queries, lengths, up_value, out_proj, residual, norm_gain, routes, route_weight, expert_gate, expert_up, expert_down):
    latent_out = lax.map(attend_sequence, (queries, latent_cache, lengths))
    head_values = jnp.einsum('shl,hlv->shv', latent_out.astype(jnp.float32), up_value.astype(jnp.float32)).astype(jnp.bfloat16)
    attended = jnp.dot(head_values.reshape(SEQS, HEADS * VDIM), out_proj.reshape(HEADS * VDIM, D), preferred_element_type=jnp.float32)
    hidden = (residual.astype(jnp.float32) + attended).astype(jnp.bfloat16)
    hidden_float = hidden.astype(jnp.float32)
    rms_scale = lax.rsqrt(lax.optimization_barrier(jnp.mean(hidden_float * hidden_float, axis=1, keepdims=True)) + 1e-06)
    normed = (hidden_float * rms_scale * norm_gain.astype(jnp.float32)[None, :]).astype(jnp.bfloat16)

    def expert_out(weights_in):
        gate_w, up_w, down_w = weights_in
        gate_pre = jnp.dot(normed, gate_w, preferred_element_type=jnp.float32)
        up_proj = jnp.dot(normed, up_w, preferred_element_type=jnp.float32)
        active = (jax.nn.silu(gate_pre) * up_proj).astype(jnp.bfloat16)
        return jnp.dot(active, down_w, preferred_element_type=jnp.float32)
    outputs = lax.map(expert_out, (expert_gate, expert_up, expert_down))
    matches = (routes[:, :, None] == jnp.arange(EXPERTS, dtype=jnp.int32)[None, None, :]).astype(jnp.float32)
    weights = lax.optimization_barrier(jnp.sum(route_weight[:, :, None] * matches, axis=1))
    combined = jnp.einsum('se,esd->sd', weights, outputs)
    return (hidden_float + combined).astype(jnp.bfloat16)
```

```python
import functools
import math

import jax
import jax.numpy as jnp
from jax import lax
from jax.experimental import pallas as pl
from jax.experimental.pallas import tpu as pltpu
from jax.sharding import PartitionSpec as P

MESH = pl.DeviceIdType.MESH
F32 = jnp.float32
BF16 = jnp.bfloat16
masked_score = -1e30
PAIR = 2
EXTRA = 128
WEIGHT_LANE = 16


def three_parts(value):
    high = value.astype(BF16).astype(F32)
    rest = value - high
    middle = rest.astype(BF16).astype(F32)
    return high, middle, (rest - middle).astype(BF16).astype(F32)


def drain(ref, sem):
    pltpu.make_async_copy(ref, ref, sem).wait()


def decode_kernel(
    side, ep, scale, width,
    lens, routes, route_w, cache, q, upv, outp, res, gain, gate, upw, down,
    out,
    kbuf, qg, obuf, st_own, st_got, lat, r1, r2_own, r2, latent,
    upg, opr, edr, gu, hv, r5_own, r5, resg, hid, u1, upl, usb, act, r8_own, r8, mix_own, mix_got,
    k_sem, own_sem, a1_s, a1_r, a2_s, a2_r, st_s, st_r, r1_s, r1_r, r2_s, r2_r,
    w_s, w_r, x_s, x_r, p_s, p_r, c_s, c_r,
):
    seq = side * side
    batch, span, _ = kbuf.shape
    chunks = batch // PAIR
    heads, lat_dim = obuf.shape[1:]
    group = heads // seq
    vdim = upv.shape[2]
    cols = opr.shape[2]
    units = gate.shape[2]
    half = ep // 2
    quarter = ep // 4
    rows_all = seq * ep

    s_me = lax.axis_index("seq")
    e_me = lax.axis_index("ep")
    x, y = lax.div(s_me, side), lax.rem(s_me, side)
    core = lax.rem(e_me, 2)
    sibling = e_me + 1 - 2 * core

    def axes(parity):
        return x + parity * (y - x), y + parity * (x - y)

    def plane(parity, a, b):
        return (a * side + b) + parity * ((b * side + a) - (a * side + b))

    def send(src, dst, send_sem, recv_sem, s, e):
        pltpu.make_async_remote_copy(
            src_ref=src, dst_ref=dst, send_sem=send_sem, recv_sem=recv_sem,
            device_id=(s, e), device_id_type=MESH,
        ).start()

    def each(lo, hi, body):
        lax.fori_loop(lo, hi, lambda i, c: (body(i), c)[1], 0)

    def other_seq(d):
        return lax.rem(s_me + d, seq)

    def other_ep(d):
        return lax.rem(e_me + d, ep)

    barrier = pltpu.get_barrier_semaphore()
    each(1, seq, lambda d: pl.semaphore_signal(
        barrier, inc=1, device_id=(other_seq(d), e_me), device_id_type=MESH))
    each(1, ep, lambda d: pl.semaphore_signal(
        barrier, inc=1, device_id=(s_me, other_ep(d)), device_id_type=MESH))

    def own_query(c):
        a, b = axes(lax.rem(c, 2))
        return pltpu.make_async_copy(
            q.at[pl.ds(c * PAIR, PAIR)], qg.at[c, a, b], own_sem.at[c])

    def load_cache(i):
        return pltpu.make_async_copy(cache.at[i], kbuf.at[i], k_sem.at[i])

    own_weights = [
        pltpu.make_async_copy(upv.at[0], upg.at[:, pl.ds(pl.multiple_of(e_me * vdim, vdim), vdim)], own_sem.at[chunks]),
        pltpu.make_async_copy(outp.at[0, :, pl.ds(pl.multiple_of(e_me * cols, cols), cols)], opr.at[e_me], own_sem.at[chunks + 1]),
        pltpu.make_async_copy(down.at[0, :, pl.ds(pl.multiple_of(e_me * cols, cols), cols)], edr.at[e_me], own_sem.at[chunks + 2]),
        pltpu.make_async_copy(gate.at[0], gu.at[:, pl.ds(0, units)], own_sem.at[chunks + 3]),
        pltpu.make_async_copy(upw.at[0], gu.at[:, pl.ds(units, units)], own_sem.at[chunks + 4]),
    ]
    each(0, chunks, lambda c: own_query(c).start())
    each(0, batch, lambda i: load_cache(i).start())
    for copy in own_weights:
        copy.start()
    resg[e_me] = res[e_me]

    pl.semaphore_wait(barrier, seq - 1 + ep - 1)

    def gather_first(c):
        parity = lax.rem(c, 2)
        a, b = axes(parity)
        for d in range(1, side):
            send(q.at[pl.ds(c * PAIR, PAIR)], qg.at[c, a, b], a1_s.at[c], a1_r.at[c],
                 plane(parity, lax.rem(a + d, side), b), e_me)

    each(0, chunks, gather_first)

    def spread(d):
        e = other_ep(d)
        here = pl.ds(pl.multiple_of(e * cols, cols), cols)
        send(upv.at[0], upg.at[:, pl.ds(pl.multiple_of(e_me * vdim, vdim), vdim)], w_s.at[0], w_r.at[0], s_me, e)
        send(outp.at[0, :, here], opr.at[e_me], w_s.at[1], w_r.at[1], s_me, e)
        send(res.at[e], resg.at[e_me], w_s.at[3], w_r.at[3], s_me, e)

    def spread_down(d):
        e = other_ep(d)
        here = pl.ds(pl.multiple_of(e * cols, cols), cols)
        send(down.at[0, :, here], edr.at[e_me], w_s.at[2], w_r.at[2], s_me, e)

    each(1, ep, spread)
    each(1, ep, spread_down)

    def gather_second(c):
        parity = lax.rem(c, 2)
        a, b = axes(parity)
        own_query(c).wait()
        drain(qg.at[c, pl.ds(0, side - 1), 0], a1_r.at[c])
        for d in range(1, side):
            send(qg.at[c, :, b], qg.at[c, :, b], a2_s.at[c], a2_r.at[c],
                 plane(parity, a, lax.rem(b + d, side)), e_me)

    eye = lax.broadcasted_iota(jnp.int32, (heads, heads), 0) == lax.broadcasted_iota(jnp.int32, (heads, heads), 1)

    def to_row(column):
        return jnp.sum(jnp.where(eye, column, 0.0), axis=0, keepdims=True)

    def to_column(row):
        return jnp.sum(jnp.where(eye, row, 0.0), axis=1, keepdims=True)

    position = s_me * span + lax.broadcasted_iota(jnp.int32, (1, span), 1)

    def attend(c):
        drain(qg.at[c, pl.ds(0, side - 1)], a2_r.at[c])
        for j in range(PAIR):
            i = c * PAIR + j
            load_cache(i).wait()
            queries = qg[c, :, :, j].astype(F32).reshape(heads, -1).astype(BF16)
            scores = lax.dot_general(queries, kbuf[i], (((1,), (1,)), ((), ())), preferred_element_type=F32)
            live = position < lens[i]
            scores = jnp.where(live, scores, masked_score)
            top = jnp.max(scores, axis=1, keepdims=True)
            prob = jnp.where(live, jnp.exp2((scores - top) * (scale * math.log2(math.e))), 0.0)
            total = jnp.sum(prob, axis=1, keepdims=True)
            obuf[i] = jnp.dot(prob.astype(BF16), kbuf[i, :, :lat_dim], preferred_element_type=F32)
            st_own[c, j:j + 1] = to_row(top)
            st_own[c, PAIR + j:PAIR + j + 1] = to_row(total)
        each(1, seq, lambda d: send(
            st_own.at[c], st_got.at[c, d - 1], st_s.at[c], st_r.at[c], other_seq(d), e_me))

    def scale_own(c):
        parity = lax.rem(c, 2)
        a, b = axes(parity)
        drain(st_got.at[c], st_r.at[c])
        own = st_own[c]
        got = st_got[c]
        own_top, own_total = own[:PAIR], own[PAIR:]
        tops, totals = got[:, :PAIR], got[:, PAIR:]
        top = jnp.maximum(own_top, jnp.max(tops, axis=0))
        own_factor = jnp.exp((own_top - top) * scale)
        den = own_total * own_factor + jnp.sum(totals * jnp.exp((tops - top[None]) * scale), axis=0)
        factor = own_factor / den
        for j in range(PAIR):
            scaled = obuf[c * PAIR + j] * to_column(factor[j:j + 1])
            lat[c, :, j] = scaled.reshape(side, side * group, lat_dim).astype(BF16)
        for d in range(1, side):
            to = lax.rem(a + d, side)
            send(lat.at[c, to], r1.at[c, d - 1], r1_s.at[c], r1_r.at[c], plane(parity, to, b), e_me)

    def sum_first(c):
        parity = lax.rem(c, 2)
        a, b = axes(parity)
        drain(r1.at[c], r1_r.at[c])
        for j in range(PAIR):
            total = lat[c, a, j].astype(F32)
            for d in range(side - 1):
                total += r1[c, d, j].astype(F32)
            r2_own[c, :, j] = total.reshape(side, group, lat_dim).astype(BF16)
        for d in range(1, side):
            to = lax.rem(b + d, side)
            send(r2_own.at[c, to], r2.at[c, d - 1], r2_s.at[c], r2_r.at[c], plane(parity, a, to), e_me)

    def sum_second(c):
        a, b = axes(lax.rem(c, 2))
        drain(r2.at[c], r2_r.at[c])
        total = r2_own[c, b].astype(F32)
        for d in range(side - 1):
            total += r2[c, d].astype(F32)
        latent[pl.ds(c * PAIR, PAIR)] = total

    ahead = 2
    each(0, min(ahead, chunks), gather_second)

    def stage(i):
        pl.when(i < chunks)(lambda: attend(i))
        pl.when(i + ahead < chunks)(lambda: gather_second(i + ahead))
        pl.when(jnp.logical_and(i >= 1, i < chunks + 1))(lambda: scale_own(i - 1))
        pl.when(jnp.logical_and(i >= 2, i < chunks + 2))(lambda: sum_first(i - 2))
        pl.when(i >= 3)(lambda: sum_second(i - 3))

    each(0, chunks + 3, stage)

    own_weights[0].wait()
    drain(upg.at[:, pl.ds(0, (ep - 1) * vdim)], w_r.at[0])
    latents = latent[...].reshape(batch * group, lat_dim).astype(BF16)
    values = jnp.dot(latents, upg[...], preferred_element_type=F32)
    row = lax.broadcasted_iota(jnp.int32, values.shape, 0)
    column = lax.broadcasted_iota(jnp.int32, values.shape, 1)
    values = jnp.where(lax.rem(row, group) == lax.div(column, vdim), values, 0.0)
    hv[e_me] = jnp.sum(values.reshape(batch, group, group * vdim), axis=1).astype(BF16)
    each(1, ep, lambda d: send(hv.at[e_me], hv.at[e_me], x_s.at[0], x_r.at[0], s_me, other_ep(d)))

    own_weights[1].wait()
    drain(opr.at[pl.ds(0, ep - 1)], w_r.at[1])
    drain(hv.at[pl.ds(0, ep - 1)], x_r.at[0])
    attended = jnp.dot(
        hv[...].reshape(rows_all, group * vdim), opr[...].reshape(ep * vdim, cols), preferred_element_type=F32)
    r5_own[...] = attended.reshape(seq, ep, cols).astype(BF16)
    each(1, seq, lambda d: send(
        r5_own.at[other_seq(d)], r5.at[d - 1], x_s.at[1], x_r.at[1], other_seq(d), e_me))

    drain(resg.at[pl.ds(0, ep - 1)], w_r.at[3])
    residual = resg[...].reshape(ep, cols)
    lane = lax.broadcasted_iota(jnp.int32, (ep, EXTRA), 1)
    sub = lax.broadcasted_iota(jnp.int32, (ep, EXTRA), 0)
    expert = lax.div(lane - WEIGHT_LANE, 3)
    part = lax.rem(lane - WEIGHT_LANE, 3)
    weight = jnp.zeros((ep, EXTRA), F32)
    for k in range(routes.shape[1]):
        weight += jnp.where(expert == routes[0, k], route_w[0, k], 0.0)
    w_high, w_mid, w_low = three_parts(weight)
    weight = jnp.where(part == 0, w_high, jnp.where(part == 1, w_mid, w_low))
    weight = jnp.where(jnp.logical_and(sub == e_me, lane >= WEIGHT_LANE), weight, 0.0)

    drain(r5, x_r.at[1])
    hidden = r5_own[s_me].astype(F32)
    for d in range(seq - 1):
        hidden += r5[d].astype(F32)
    hidden = (hidden + residual).astype(BF16).astype(F32)
    hid[...] = hidden
    s_high, s_mid, s_low = three_parts(jnp.sum(hidden * hidden, axis=1, keepdims=True))
    squares = jnp.where(lane == 0, s_high, jnp.where(lane == 1, s_mid, jnp.where(lane == 2, s_low, 0.0)))
    u1[e_me, :, :cols] = (hidden * gain[e_me]).astype(BF16)
    u1[e_me, :, cols:] = (squares + weight).astype(BF16)
    each(1, ep, lambda d: send(u1.at[e_me], u1.at[e_me], x_s.at[2], x_r.at[2], s_me, other_ep(d)))

    drain(u1.at[pl.ds(0, ep - 1)], x_r.at[2])
    for t in range(2):
        a, b = axes(t)
        upl[t, a, b] = u1[pl.ds(core * half + t * quarter, quarter)]
        for d in range(1, side):
            send(upl.at[t, a, b], upl.at[t, a, b], p_s.at[t], p_r.at[t], plane(t, lax.rem(a + d, side), b), e_me)
    for t in range(2):
        a, b = axes(t)
        drain(upl.at[t, pl.ds(0, side - 1), 0], p_r.at[t])
        for d in range(1, side):
            send(upl.at[t, :, b], upl.at[t, :, b], p_s.at[2 + t], p_r.at[2 + t], plane(t, a, lax.rem(b + d, side)), e_me)
    for t in range(2):
        drain(upl.at[t, pl.ds(0, side - 1)], p_r.at[2 + t])
        send(upl.at[t], usb.at[t], c_s.at[t], c_r.at[t], s_me, sibling)

    own_weights[3].wait()
    own_weights[4].wait()
    gated = jnp.zeros((rows_all, 2 * units), F32)
    extra = jnp.zeros((rows_all, EXTRA), F32)
    for which in range(2):
        for t in range(2):
            buf = (upl, usb)[which]
            if which:
                drain(usb.at[t], c_r.at[t])
            first = (core + which * (1 - 2 * core)) * half + t * quarter
            for k in range(quarter):
                rows = [
                    (buf[t, i, j, k] if t == 0 else buf[t, j, i, k]).astype(F32)
                    for i in range(side) for j in range(side)
                ]
                rows = jnp.concatenate(rows, axis=0)
                at = pl.ds(pl.multiple_of((first + k) * cols, cols), cols)
                gated += jnp.dot(rows[:, :cols].astype(BF16), gu[at, :], preferred_element_type=F32)
                extra += rows[:, cols:]

    lane = lax.broadcasted_iota(jnp.int32, extra.shape, 1)
    mine = WEIGHT_LANE + 3 * s_me
    squares = jnp.sum(jnp.where(lane < 3, extra, 0.0), axis=1, keepdims=True)
    weight = jnp.sum(jnp.where(jnp.logical_and(lane >= mine, lane < mine + 3), extra, 0.0), axis=1, keepdims=True)
    rms = lax.rsqrt(squares / width + 1e-6)
    gated = gated * rms
    gate_pre, up_pre = gated[:, :units], gated[:, units:]
    act[e_me] = (gate_pre / (1.0 + jnp.exp(-gate_pre)) * up_pre).astype(BF16)
    each(1, ep, lambda d: send(act.at[e_me], act.at[e_me], x_s.at[3], x_r.at[3], s_me, other_ep(d)))

    own_weights[2].wait()
    drain(edr.at[pl.ds(0, ep - 1)], w_r.at[2])
    drain(act.at[pl.ds(0, ep - 1)], x_r.at[3])
    acts = jnp.concatenate([act[e] for e in range(ep)], axis=1)
    result = jnp.dot(acts, edr[...].reshape(ep * units, cols), preferred_element_type=F32) * weight
    r8_own[...] = result.reshape(seq, ep, cols).astype(BF16)
    each(1, seq, lambda d: send(
        r8_own.at[other_seq(d)], r8.at[d - 1], x_s.at[4], x_r.at[4], other_seq(d), e_me))

    drain(r8, x_r.at[4])
    mixed = r8_own[s_me].astype(F32)
    for d in range(seq - 1):
        mixed += r8[d].astype(F32)
    mixed = mixed + hid[...]
    mix_own[...] = mixed.reshape(ep, 1, cols)
    mix_got[e_me] = mix_own[e_me]
    each(1, ep, lambda d: send(
        mix_own.at[other_ep(d)], mix_got.at[e_me], x_s.at[5], x_r.at[5], s_me, other_ep(d)))
    drain(mix_got.at[pl.ds(0, ep - 1)], x_r.at[5])
    out[...] = mix_got[...]

    def sent(c):
        drain(qg.at[c, pl.ds(0, side - 1), 0], a1_s.at[c])
        drain(qg.at[c, pl.ds(0, side - 1)], a2_s.at[c])
        drain(st_got.at[c], st_s.at[c])
        drain(r1.at[c], r1_s.at[c])
        drain(r2.at[c], r2_s.at[c])

    each(0, chunks, sent)
    drain(upg.at[:, pl.ds(0, (ep - 1) * vdim)], w_s.at[0])
    drain(opr.at[pl.ds(0, ep - 1)], w_s.at[1])
    drain(edr.at[pl.ds(0, ep - 1)], w_s.at[2])
    drain(resg.at[pl.ds(0, ep - 1)], w_s.at[3])
    drain(hv.at[pl.ds(0, ep - 1)], x_s.at[0])
    drain(r5, x_s.at[1])
    drain(u1.at[pl.ds(0, ep - 1)], x_s.at[2])
    drain(act.at[pl.ds(0, ep - 1)], x_s.at[3])
    drain(r8, x_s.at[4])
    drain(mix_got.at[pl.ds(0, ep - 1)], x_s.at[5])
    for t in range(2):
        drain(upl.at[t, pl.ds(0, side - 1), 0], p_s.at[t])
        drain(upl.at[t, pl.ds(0, side - 1)], p_s.at[2 + t])
        drain(usb.at[t], c_s.at[t])


def shards(
    seq, ep, latent_cache, queries, lengths, up_value, out_proj, residual, norm_gain,
    routes, route_weight, expert_gate, expert_up, expert_down,
):
    side = math.isqrt(seq)
    batch, span, kdim = latent_cache.shape
    group = queries.shape[1]
    heads = group * seq
    lat_dim, vdim = up_value.shape[1:]
    width = residual.shape[1]
    cols = width // ep
    units = expert_gate.shape[2]
    chunks = batch // PAIR
    rows_all = seq * ep
    dma = pltpu.SemaphoreType.DMA
    vmem = pltpu.VMEM
    scratch = [
        vmem((batch, span, kdim), BF16),
        vmem((chunks, side, side, PAIR, group, kdim), BF16),
        vmem((batch, heads, lat_dim), F32),
        vmem((chunks, 2 * PAIR, heads), F32),
        vmem((chunks, seq - 1, 2 * PAIR, heads), F32),
        vmem((chunks, side, PAIR, side * group, lat_dim), BF16),
        vmem((chunks, side - 1, PAIR, side * group, lat_dim), BF16),
        vmem((chunks, side, PAIR, group, lat_dim), BF16),
        vmem((chunks, side - 1, PAIR, group, lat_dim), BF16),
        vmem((batch, group, lat_dim), F32),
        vmem((lat_dim, ep * vdim), BF16),
        vmem((ep, vdim, cols), BF16),
        vmem((ep, units, cols), BF16),
        vmem((width, 2 * units), BF16),
        vmem((ep, batch, group * vdim), BF16),
        vmem((seq, ep, cols), BF16),
        vmem((seq - 1, ep, cols), BF16),
        vmem((ep, 1, cols), F32),
        vmem((ep, cols), F32),
        vmem((ep, ep, cols + EXTRA), BF16),
        vmem((2, side, side, ep // 4, ep, cols + EXTRA), BF16),
        vmem((2, side, side, ep // 4, ep, cols + EXTRA), BF16),
        vmem((ep, rows_all, units), BF16),
        vmem((seq, ep, cols), BF16),
        vmem((seq - 1, ep, cols), BF16),
        vmem((ep, 1, cols), F32),
        vmem((ep, 1, cols), F32),
        dma((batch,)),
        dma((chunks + 5,)),
    ]
    scratch += [dma((chunks,)) for _ in range(10)]
    scratch += [dma((4,)), dma((4,)), dma((6,)), dma((6,)), dma((4,)), dma((4,)), dma((2,)), dma((2,))]
    smem = pl.BlockSpec(memory_space=pltpu.SMEM)
    whole = pl.BlockSpec(memory_space=pltpu.VMEM)
    anywhere = pl.BlockSpec(memory_space=pl.ANY)
    mixed = pl.pallas_call(
        functools.partial(decode_kernel, side, ep, 192.0 ** (-0.5), width),
        out_shape=jax.ShapeDtypeStruct((ep, 1, cols), F32),
        in_specs=[smem, smem, smem] + [anywhere] * 4 + [whole, whole] + [anywhere] * 3,
        out_specs=whole,
        scratch_shapes=scratch,
        compiler_params=pltpu.CompilerParams(
            collective_id=0, has_side_effects=True, vmem_limit_bytes=58 * 1024 * 1024),
        name="decode",
    )(
        lengths, routes, route_weight, latent_cache, queries, up_value, out_proj,
        residual.astype(F32).reshape(ep, 1, cols), norm_gain.astype(F32).reshape(ep, 1, cols),
        expert_gate, expert_up, expert_down,
    )
    return mixed.reshape(1, width).astype(BF16)


def solution(mesh):
    placed = (
        P("ep", "seq", None),
        P("ep", "seq", None),
        P("ep"),
        P(("seq", "ep"), None, None),
        P(("seq", "ep"), None, None),
        P(("seq", "ep"), None),
        P(),
        P(("seq", "ep"), None),
        P(("seq", "ep"), None),
        P("seq", None, "ep"),
        P("seq", None, "ep"),
        P("seq", "ep", None),
    )
    return jax.shard_map(
        functools.partial(shards, mesh.shape["seq"], mesh.shape["ep"]),
        mesh=mesh, in_specs=placed, out_specs=P(("seq", "ep"), None), check_vma=False,
    )
```

```python
import functools
import math

import jax
import jax.numpy as jnp
from jax import lax
from jax.experimental import pallas as pl
from jax.experimental.pallas import tpu as pltpu
from jax.sharding import PartitionSpec as P

MESH = pl.DeviceIdType.MESH
F32 = jnp.float32
BF16 = jnp.bfloat16
masked_score = -1e30
PAIR = 2
LANES = 128
EXTRA = LANES
WEIGHT_LANE = 16


def three_parts(value):
    high = value.astype(BF16).astype(F32)
    rest = value - high
    middle = rest.astype(BF16).astype(F32)
    return high, middle, (rest - middle).astype(BF16).astype(F32)


def drain(ref, sem):
    pltpu.make_async_copy(ref, ref, sem).wait()


def decode_kernel(
    side, ep, scale, width,
    lens, routes, route_w, cache, q, upv, outp, res, gain, gate, upw, down,
    out,
    kbuf, qg, st1_own, st1, lat, r1, st2_own, st2, r2_own, r2, latent, res32, gain32,
    upg, opr, edr, gu, hv, r5_own, r5, resg, hid, u1, upl, usb, act, r8_own, r8, mix_own, mix_got,
    k_sem, own_sem, a1_s, a1_r, a2_s, a2_r, st1_s, st1_r, st2_s, st2_r, r1_s, r1_r, r2_s, r2_r,
    w_s, w_r, x_s, x_r, p_s, p_r, c_s, c_r,
):
    seq = side * side
    batch, _, span = kbuf.shape
    chunks = batch // PAIR
    group, lat_dim = latent.shape[1:]
    heads = group * seq
    vdim = upv.shape[2]
    cols = opr.shape[2]
    units = gate.shape[2]
    half = ep // 2
    quarter = ep // 4
    rows_all = seq * ep

    s_me = lax.axis_index("seq")
    e_me = lax.axis_index("ep")
    x, y = lax.div(s_me, side), lax.rem(s_me, side)
    z, core = lax.div(e_me, 2), lax.rem(e_me, 2)
    sibling = e_me + 1 - 2 * core

    def axes(parity):
        return x + parity * (y - x), y + parity * (x - y)

    def plane(parity, a, b):
        return (a * side + b) + parity * ((b * side + a) - (a * side + b))

    def send(src, dst, send_sem, recv_sem, s, e):
        pltpu.make_async_remote_copy(
            src_ref=src, dst_ref=dst, send_sem=send_sem, recv_sem=recv_sem,
            device_id=(s, e), device_id_type=MESH,
        ).start()

    def each(lo, hi, body):
        lax.fori_loop(lo, hi, lambda i, c: (body(i), c)[1], 0)

    def other_seq(d):
        return lax.rem(s_me + d, seq)

    def other_ep(d):
        return lax.rem(e_me + d, ep)

    left = []

    def finish():
        for wait in left:
            wait()

    barrier = pltpu.get_barrier_semaphore()
    each(1, side, lambda d: pl.semaphore_signal(
        barrier, inc=1, device_id=(plane(0, lax.rem(x + d, side), y), e_me), device_id_type=MESH))
    each(1, side, lambda d: pl.semaphore_signal(
        barrier, inc=1, device_id=(plane(0, x, lax.rem(y + d, side)), e_me), device_id_type=MESH))
    each(1, ep, lambda d: pl.semaphore_signal(
        barrier, inc=1, device_id=(s_me, other_ep(d)), device_id_type=MESH))

    def own_query(c):
        a, b = axes(lax.rem(c, 2))
        return pltpu.make_async_copy(
            q.at[pl.ds(c * PAIR, PAIR)], qg.at[c, a, b], own_sem.at[c])

    def load_cache(i):
        return pltpu.make_async_copy(cache.at[i], kbuf.at[i], k_sem.at[i])

    slot = core * half + z
    values_here = pl.ds(pl.multiple_of(z * vdim, vdim), vdim)
    own_weights = [
        pltpu.make_async_copy(upv.at[0], upg.at[core, :, values_here], own_sem.at[chunks]),
        pltpu.make_async_copy(outp.at[0, :, pl.ds(pl.multiple_of(e_me * cols, cols), cols)], opr.at[slot], own_sem.at[chunks + 1]),
        pltpu.make_async_copy(down.at[0, :, pl.ds(pl.multiple_of(e_me * cols, cols), cols)], edr.at[e_me], own_sem.at[chunks + 2]),
        pltpu.make_async_copy(gate.at[0], gu.at[:, pl.ds(0, units)], own_sem.at[chunks + 3]),
        pltpu.make_async_copy(upw.at[0], gu.at[:, pl.ds(units, units)], own_sem.at[chunks + 4]),
    ]
    each(0, chunks, lambda c: own_query(c).start())
    each(0, batch, lambda i: load_cache(i).start())
    for copy in own_weights:
        copy.start()
    res32[...] = res[...].astype(F32)
    gain32[...] = gain[...].astype(F32)
    resg[e_me] = res32[e_me]

    pl.semaphore_wait(barrier, 2 * (side - 1) + ep - 1)

    def gather_first(c):
        parity = lax.rem(c, 2)
        a, b = axes(parity)
        for d in range(1, side):
            send(q.at[pl.ds(c * PAIR, PAIR)], qg.at[c, a, b], a1_s.at[c], a1_r.at[c],
                 plane(parity, lax.rem(a + d, side), b), e_me)

    each(0, chunks, gather_first)
    left.append(lambda: each(0, chunks, lambda c: drain(qg.at[c, pl.ds(0, side - 1), 0], a1_s.at[c])))

    def spread_values(d):
        send(upv.at[0], upg.at[core, :, values_here], w_s.at[0], w_r.at[0], s_me, lax.rem(z + d, half) * 2 + core)

    def forward_values():
        own_weights[0].wait()
        drain(upg.at[0, :, pl.ds(0, (half - 1) * vdim)], w_r.at[0])
        send(upg.at[core], upg.at[core], c_s.at[2], c_r.at[2], s_me, sibling)

    def spread(d):
        e = other_ep(d)
        here = pl.ds(pl.multiple_of(e * cols, cols), cols)
        send(outp.at[0, :, here], opr.at[slot], w_s.at[1], w_r.at[1], s_me, e)
        send(res32.at[e], resg.at[e_me], w_s.at[3], w_r.at[3], s_me, e)

    def spread_down(hop, flip):
        e = lax.rem(z + hop, half) * 2 + lax.rem(core + flip, 2)
        here = pl.ds(pl.multiple_of(e * cols, cols), cols)
        send(down.at[0, :, here], edr.at[e_me], w_s.at[2], w_r.at[2], s_me, e)

    far = half // 2
    each(1, half, spread_values)
    each(1, ep, spread)
    spread_down(0, 1)
    for hop in range(1, half):
        if hop != far:
            spread_down(hop, 0)
            spread_down(hop, 1)

    left.append(lambda: drain(upg.at[0, :, pl.ds(0, (half - 1) * vdim)], w_s.at[0]))
    left.append(lambda: drain(opr.at[pl.ds(0, ep - 1)], w_s.at[1]))
    left.append(lambda: drain(resg.at[pl.ds(0, ep - 1)], w_s.at[3]))

    def gather_second(c):
        parity = lax.rem(c, 2)
        a, b = axes(parity)
        own_query(c).wait()
        drain(qg.at[c, pl.ds(0, side - 1), 0], a1_r.at[c])
        for d in range(1, side):
            send(qg.at[c, :, b], qg.at[c, :, b], a2_s.at[c], a2_r.at[c],
                 plane(parity, a, lax.rem(b + d, side)), e_me)

    def diagonal(rows, first):
        lane = lax.broadcasted_iota(jnp.int32, (rows, heads), 1)
        return lane == first + lax.broadcasted_iota(jnp.int32, (rows, heads), 0)

    eye = diagonal(heads, 0)

    def to_column(row, mask):
        return jnp.sum(jnp.where(mask, row, 0.0), axis=1, keepdims=True)

    position = s_me * span + lax.broadcasted_iota(jnp.int32, (1, span), 1)

    def attend(c):
        drain(qg.at[c, pl.ds(0, side - 1)], a2_r.at[c])
        for j in range(PAIR):
            i = c * PAIR + j
            load_cache(i).wait()
            queries = qg[c, :, :, j].astype(F32).reshape(heads, -1).astype(BF16)
            scores = jnp.dot(queries, kbuf[i], preferred_element_type=F32)
            live = position < lens[i]
            scores = jnp.where(live, scores, masked_score)
            top = jnp.max(scores, axis=1, keepdims=True)
            prob = jnp.where(live, jnp.exp2((scores - top) * (scale * math.log2(math.e))), 0.0)
            total = jnp.sum(prob, axis=1, keepdims=True)
            total = jnp.maximum(total, 1.0)
            mean = lax.dot_general(
                prob.astype(BF16), kbuf[i, :lat_dim], (((1,), (1,)), ((), ())), preferred_element_type=F32) / total
            lat[c, :, j] = mean.reshape(side, side * group, lat_dim).astype(BF16)
            level = top * scale + jnp.log(total)
            st1_own[c, j:j + 1] = jnp.sum(jnp.where(eye, level, 0.0), axis=0, keepdims=True)
        parity = lax.rem(c, 2)
        a, b = axes(parity)
        for d in range(1, side):
            to = lax.rem(a + d, side)
            send(st1_own.at[c], st1.at[c, d - 1], st1_s.at[c], st1_r.at[c], plane(parity, to, b), e_me)
            send(lat.at[c, to], r1.at[c, d - 1], r1_s.at[c], r1_r.at[c], plane(parity, to, b), e_me)

    def merge(own_level, levels):
        top = jnp.maximum(own_level, jnp.max(levels, axis=0))
        weights = [jnp.exp(own_level - top)] + [jnp.exp(levels[d] - top) for d in range(side - 1)]
        den = sum(weights)
        return top + jnp.log(den), [w / den for w in weights]

    def sum_first(c):
        parity = lax.rem(c, 2)
        a, b = axes(parity)
        drain(st1.at[c], st1_r.at[c])
        level, weights = merge(st1_own[c], st1[c])
        st2_own[c] = level
        mask = diagonal(side * group, a * side * group)
        drain(r1.at[c], r1_r.at[c])
        for j in range(PAIR):
            total = lat[c, a, j].astype(F32) * to_column(weights[0][j:j + 1], mask)
            for d in range(side - 1):
                total += r1[c, d, j].astype(F32) * to_column(weights[d + 1][j:j + 1], mask)
            r2_own[c, :, j] = total.reshape(side, group, lat_dim).astype(BF16)
        for d in range(1, side):
            to = lax.rem(b + d, side)
            send(st2_own.at[c], st2.at[c, d - 1], st2_s.at[c], st2_r.at[c], plane(parity, a, to), e_me)
            send(r2_own.at[c, to], r2.at[c, d - 1], r2_s.at[c], r2_r.at[c], plane(parity, a, to), e_me)

    def sum_second(c):
        a, b = axes(lax.rem(c, 2))
        drain(st2.at[c], st2_r.at[c])
        _, weights = merge(st2_own[c], st2[c])
        mask = diagonal(group, (a * side + b) * group)
        drain(r2.at[c], r2_r.at[c])
        for j in range(PAIR):
            total = r2_own[c, b, j].astype(F32) * to_column(weights[0][j:j + 1], mask)
            for d in range(side - 1):
                total += r2[c, d, j].astype(F32) * to_column(weights[d + 1][j:j + 1], mask)
            latent[c * PAIR + j] = total

    each(0, chunks, gather_second)
    lag = 3

    def stage(i):
        pl.when(i == chunks // 2)(forward_values)

        def at(step, low):
            c = i - low * lag
            pl.when(jnp.logical_and(c >= 0, c < chunks))(lambda: step(c))

        at(attend, 0)
        at(sum_first, 1)
        at(sum_second, 2)

    each(0, chunks + 2 * lag, stage)

    def sent(c):
        drain(qg.at[c, pl.ds(0, side - 1)], a2_s.at[c])
        drain(st1.at[c], st1_s.at[c])
        drain(st2.at[c], st2_s.at[c])
        drain(r1.at[c], r1_s.at[c])
        drain(r2.at[c], r2_s.at[c])

    left.append(lambda: each(0, chunks, sent))
    left.append(lambda: drain(upg.at[0], c_s.at[2]))

    drain(upg.at[0], c_r.at[2])
    latents = latent[...].reshape(batch * group, lat_dim).astype(BF16)
    values = jnp.concatenate(
        [jnp.dot(latents, upg[k], preferred_element_type=F32) for k in range(2)], axis=1)
    row = lax.broadcasted_iota(jnp.int32, values.shape, 0)
    block = lax.div(lax.broadcasted_iota(jnp.int32, values.shape, 1), vdim)
    values = jnp.where(lax.rem(row, group) == lax.rem(block, half) * 2 + lax.div(block, half), values, 0.0)
    hv[e_me] = jnp.sum(values.reshape(batch, group, group * vdim), axis=1).astype(BF16)
    each(1, ep, lambda d: send(hv.at[e_me], hv.at[e_me], x_s.at[0], x_r.at[0], s_me, other_ep(d)))
    left.append(lambda: drain(hv.at[pl.ds(0, ep - 1)], x_s.at[0]))

    own_weights[1].wait()
    drain(opr.at[pl.ds(0, ep - 1)], w_r.at[1])
    drain(hv.at[pl.ds(0, ep - 1)], x_r.at[0])
    attended = jnp.dot(
        hv[...].reshape(rows_all, group * vdim), opr[...].reshape(ep * vdim, cols), preferred_element_type=F32)
    r5_own[...] = attended.reshape(seq, ep, cols).astype(BF16)
    each(1, seq, lambda d: send(
        r5_own.at[other_seq(d)], r5.at[d - 1], x_s.at[1], x_r.at[1], other_seq(d), e_me))
    left.append(lambda: drain(r5, x_s.at[1]))

    drain(resg.at[pl.ds(0, ep - 1)], w_r.at[3])
    residual = resg[...].reshape(ep, cols)
    lane = lax.broadcasted_iota(jnp.int32, (ep, EXTRA), 1)
    sub = lax.broadcasted_iota(jnp.int32, (ep, EXTRA), 0)
    expert = lax.div(lane - WEIGHT_LANE, 3)
    part = lax.rem(lane - WEIGHT_LANE, 3)
    weight = jnp.zeros((ep, EXTRA), F32)
    for k in range(routes.shape[1]):
        weight += jnp.where(expert == routes[0, k], route_w[0, k], 0.0)
    w_high, w_mid, w_low = three_parts(weight)
    weight = jnp.where(part == 0, w_high, jnp.where(part == 1, w_mid, w_low))
    weight = jnp.where(jnp.logical_and(sub == e_me, lane >= WEIGHT_LANE), weight, 0.0)

    drain(r5, x_r.at[1])
    hidden = r5_own[s_me].astype(F32)
    for d in range(seq - 1):
        hidden += r5[d].astype(F32)
    hidden = (hidden + residual).astype(BF16).astype(F32)
    hid[...] = hidden
    s_high, s_mid, s_low = three_parts(jnp.sum(hidden * hidden, axis=1, keepdims=True))
    squares = jnp.where(lane == 0, s_high, jnp.where(lane == 1, s_mid, jnp.where(lane == 2, s_low, 0.0)))
    per = cols // LANES
    gain_row = jnp.concatenate([gain32[pl.ds(e_me * per + k, 1), :] for k in range(per)], axis=1)
    u1[e_me, :, :cols] = (hidden * gain_row).astype(BF16)
    u1[e_me, :, cols:] = (squares + weight).astype(BF16)
    each(1, ep, lambda d: send(u1.at[e_me], u1.at[e_me], x_s.at[2], x_r.at[2], s_me, other_ep(d)))
    left.append(lambda: drain(u1.at[pl.ds(0, ep - 1)], x_s.at[2]))

    drain(u1.at[pl.ds(0, ep - 1)], x_r.at[2])
    spread_down(far, 0)
    spread_down(far, 1)
    left.append(lambda: drain(edr.at[pl.ds(0, ep - 1)], w_s.at[2]))
    for t in range(2):
        a, b = axes(t)
        upl[t, a, b] = u1[pl.ds(core * half + t * quarter, quarter)]
        for d in range(1, side):
            send(upl.at[t, a, b], upl.at[t, a, b], p_s.at[t], p_r.at[t], plane(t, lax.rem(a + d, side), b), e_me)
    for t in range(2):
        a, b = axes(t)
        drain(upl.at[t, pl.ds(0, side - 1), 0], p_r.at[t])
        for d in range(1, side):
            send(upl.at[t, :, b], upl.at[t, :, b], p_s.at[2 + t], p_r.at[2 + t], plane(t, a, lax.rem(b + d, side)), e_me)
    for t in range(2):
        drain(upl.at[t, pl.ds(0, side - 1)], p_r.at[2 + t])
        send(upl.at[t], usb.at[t], c_s.at[t], c_r.at[t], s_me, sibling)

    def sent_rows():
        for t in range(2):
            drain(upl.at[t, pl.ds(0, side - 1), 0], p_s.at[t])
            drain(upl.at[t, pl.ds(0, side - 1)], p_s.at[2 + t])
            drain(usb.at[t], c_s.at[t])

    left.append(sent_rows)

    own_weights[3].wait()
    own_weights[4].wait()
    gated = jnp.zeros((rows_all, 2 * units), F32)
    extra = jnp.zeros((rows_all, EXTRA), F32)
    for which in range(2):
        for t in range(2):
            buf = (upl, usb)[which]
            if which:
                drain(usb.at[t], c_r.at[t])
            first = (core + which * (1 - 2 * core)) * half + t * quarter
            for k in range(quarter):
                rows = [
                    (buf[t, i, j, k] if t == 0 else buf[t, j, i, k]).astype(F32)
                    for i in range(side) for j in range(side)
                ]
                rows = jnp.concatenate(rows, axis=0)
                at = pl.ds(pl.multiple_of((first + k) * cols, cols), cols)
                gated += jnp.dot(rows[:, :cols].astype(BF16), gu[at, :], preferred_element_type=F32)
                extra += rows[:, cols:]

    lane = lax.broadcasted_iota(jnp.int32, extra.shape, 1)
    mine = WEIGHT_LANE + 3 * s_me
    squares = jnp.sum(jnp.where(lane < 3, extra, 0.0), axis=1, keepdims=True)
    weight = jnp.sum(jnp.where(jnp.logical_and(lane >= mine, lane < mine + 3), extra, 0.0), axis=1, keepdims=True)
    rms = lax.rsqrt(squares / width + 1e-6)
    gated = gated * rms
    gate_pre, up_pre = gated[:, :units], gated[:, units:]
    act[e_me] = (gate_pre / (1.0 + jnp.exp(-gate_pre)) * up_pre).astype(BF16)
    each(1, ep, lambda d: send(act.at[e_me], act.at[e_me], x_s.at[3], x_r.at[3], s_me, other_ep(d)))
    left.append(lambda: drain(act.at[pl.ds(0, ep - 1)], x_s.at[3]))

    own_weights[2].wait()
    drain(edr.at[pl.ds(0, ep - 1)], w_r.at[2])
    drain(act.at[pl.ds(0, ep - 1)], x_r.at[3])
    acts = jnp.concatenate([act[e] for e in range(ep)], axis=1)
    result = jnp.dot(acts, edr[...].reshape(ep * units, cols), preferred_element_type=F32) * weight
    r8_own[...] = result.reshape(seq, ep, cols).astype(BF16)
    each(1, seq, lambda d: send(
        r8_own.at[other_seq(d)], r8.at[d - 1], x_s.at[4], x_r.at[4], other_seq(d), e_me))
    left.append(lambda: drain(r8, x_s.at[4]))

    drain(r8, x_r.at[4])
    mixed = r8_own[s_me].astype(F32)
    for d in range(seq - 1):
        mixed += r8[d].astype(F32)
    mixed = mixed + hid[...]
    mix_own[...] = mixed.reshape(ep, 1, cols)
    mix_got[e_me] = mix_own[e_me]
    each(1, ep, lambda d: send(
        mix_own.at[other_ep(d)], mix_got.at[e_me], x_s.at[5], x_r.at[5], s_me, other_ep(d)))
    left.append(lambda: drain(mix_got.at[pl.ds(0, ep - 1)], x_s.at[5]))
    drain(mix_got.at[pl.ds(0, ep - 1)], x_r.at[5])
    out[...] = mix_got[...]

    finish()


def shards(
    seq, ep, latent_cache, queries, lengths, up_value, out_proj, residual, norm_gain,
    routes, route_weight, expert_gate, expert_up, expert_down,
):
    side = math.isqrt(seq)
    batch, span, kdim = latent_cache.shape
    group = queries.shape[1]
    heads = group * seq
    lat_dim, vdim = up_value.shape[1:]
    width = residual.shape[1]
    cols = width // ep
    units = expert_gate.shape[2]
    chunks = batch // PAIR
    rows_all = seq * ep
    dma = pltpu.SemaphoreType.DMA
    vmem = pltpu.VMEM
    scratch = [
        vmem((batch, kdim, span), BF16),
        vmem((chunks, side, side, PAIR, group, kdim), BF16),
        vmem((chunks, PAIR, heads), F32),
        vmem((chunks, side - 1, PAIR, heads), F32),
        vmem((chunks, side, PAIR, side * group, lat_dim), BF16),
        vmem((chunks, side - 1, PAIR, side * group, lat_dim), BF16),
        vmem((chunks, PAIR, heads), F32),
        vmem((chunks, side - 1, PAIR, heads), F32),
        vmem((chunks, side, PAIR, group, lat_dim), BF16),
        vmem((chunks, side - 1, PAIR, group, lat_dim), BF16),
        vmem((batch, group, lat_dim), F32),
        vmem((ep, 1, cols), F32),
        vmem((width // LANES, LANES), F32),
        vmem((2, lat_dim, ep // 2 * vdim), BF16),
        vmem((ep, vdim, cols), BF16),
        vmem((ep, units, cols), BF16),
        vmem((width, 2 * units), BF16),
        vmem((ep, batch, group * vdim), BF16),
        vmem((seq, ep, cols), BF16),
        vmem((seq - 1, ep, cols), BF16),
        vmem((ep, 1, cols), F32),
        vmem((ep, cols), F32),
        vmem((ep, ep, cols + EXTRA), BF16),
        vmem((2, side, side, ep // 4, ep, cols + EXTRA), BF16),
        vmem((2, side, side, ep // 4, ep, cols + EXTRA), BF16),
        vmem((ep, rows_all, units), BF16),
        vmem((seq, ep, cols), BF16),
        vmem((seq - 1, ep, cols), BF16),
        vmem((ep, 1, cols), F32),
        vmem((ep, 1, cols), F32),
        dma((batch,)),
        dma((chunks + 5,)),
    ]
    scratch += [dma((chunks,)) for _ in range(12)]
    scratch += [dma((4,)), dma((4,)), dma((6,)), dma((6,)), dma((4,)), dma((4,)), dma((3,)), dma((3,))]
    smem = pl.BlockSpec(memory_space=pltpu.SMEM)
    whole = pl.BlockSpec(memory_space=pltpu.VMEM)
    anywhere = pl.BlockSpec(memory_space=pl.ANY)
    mixed = pl.pallas_call(
        functools.partial(decode_kernel, side, ep, 192.0 ** (-0.5), width),
        out_shape=jax.ShapeDtypeStruct((ep, 1, cols), F32),
        in_specs=[smem, smem, smem] + [anywhere] * 4 + [whole, whole] + [anywhere] * 3,
        out_specs=whole,
        scratch_shapes=scratch,
        compiler_params=pltpu.CompilerParams(
            collective_id=0, has_side_effects=True, vmem_limit_bytes=58 * 1024 * 1024),
        name="decode",
    )(
        lengths, routes, route_weight, jnp.swapaxes(latent_cache, 1, 2), queries, up_value, out_proj,
        residual.reshape(ep, 1, cols), norm_gain.reshape(width // LANES, LANES),
        expert_gate, expert_up, expert_down,
    )
    return mixed.reshape(1, width).astype(BF16)


def solution(mesh):
    placed = (
        P("ep", "seq", None),
        P("ep", "seq", None),
        P("ep"),
        P(("seq", "ep"), None, None),
        P(("seq", "ep"), None, None),
        P(("seq", "ep"), None),
        P(),
        P(("seq", "ep"), None),
        P(("seq", "ep"), None),
        P("seq", None, "ep"),
        P("seq", None, "ep"),
        P("seq", "ep", None),
    )
    return jax.shard_map(
        functools.partial(shards, mesh.shape["seq"], mesh.shape["ep"]),
        mesh=mesh, in_specs=placed, out_specs=P(("seq", "ep"), None), check_vma=False,
    )
```

```python
import functools
import math

import jax
import jax.numpy as jnp
from jax import lax
from jax.experimental import pallas as pl
from jax.experimental.pallas import tpu as pltpu
from jax.sharding import PartitionSpec as P

MESH = pl.DeviceIdType.MESH
F32 = jnp.float32
BF16 = jnp.bfloat16
masked_score = -1e30
PAIR = 2
LANES = 128
EXTRA = LANES
WEIGHT_LANE = 16


def three_parts(value):
    high = value.astype(BF16).astype(F32)
    rest = value - high
    middle = rest.astype(BF16).astype(F32)
    return high, middle, (rest - middle).astype(BF16).astype(F32)


def row_cuts(cols):
    tiles = (cols + EXTRA) // LANES
    return [LANES * (tiles * p // 3) for p in range(3)] + [cols + EXTRA]


def drain(ref, sem):
    pltpu.make_async_copy(ref, ref, sem).wait()


def decode_kernel(
    side, ep, scale, width,
    lens, routes, route_w, cache, q, upv, outp, res, gain, gate, upw, down,
    out,
    kbuf, qraw, qg, st1_own, st1, lat, r1, st2_own, st2, r2_own, r2, latent, res32, gain32,
    upg, opr, edr, gu, hv, r5_own, r5, resg, hid, rows_a, rows_b, rows_c, rows_oa, rows_ob, rows_oc, act, r8_own, r8, mix_own, mix_got,
    k_sem, own_sem, a1_s, a1_r, a2_s, a2_r, a3_s, a3_r, st1_s, st1_r, st2_s, st2_r, r1_s, r1_r, r2_s, r2_r,
    w_s, w_r, x_s, x_r, p_s, p_r, c_s, c_r, h_s, h_r,
):
    seq = side * side
    batch, _, span = kbuf.shape
    chunks = batch // PAIR
    group, lat_dim = latent.shape[1:]
    heads = group * seq
    vdim = upv.shape[2]
    cols = opr.shape[2]
    units = gate.shape[2]
    half = ep // 2
    rows_all = seq * ep

    s_me = lax.axis_index("seq")
    e_me = lax.axis_index("ep")
    x, y = lax.div(s_me, side), lax.rem(s_me, side)
    z, core = lax.div(e_me, 2), lax.rem(e_me, 2)
    sibling = e_me + 1 - 2 * core

    def axes(parity):
        return x + parity * (y - x), y + parity * (x - y)

    def plane(parity, a, b):
        return (a * side + b) + parity * ((b * side + a) - (a * side + b))

    def send(src, dst, send_sem, recv_sem, s, e):
        pltpu.make_async_remote_copy(
            src_ref=src, dst_ref=dst, send_sem=send_sem, recv_sem=recv_sem,
            device_id=(s, e), device_id_type=MESH,
        ).start()

    def each(lo, hi, body):
        lax.fori_loop(lo, hi, lambda i, c: (body(i), c)[1], 0)

    def other_seq(d):
        return lax.rem(s_me + d, seq)

    def other_ep(d):
        return lax.rem(e_me + d, ep)

    cuts = row_cuts(cols)
    rows_p, rows_o = (rows_a, rows_b, rows_c), (rows_oa, rows_ob, rows_oc)
    left = []

    def finish():
        for wait in left:
            wait()

    barrier = pltpu.get_barrier_semaphore()
    each(1, side, lambda d: pl.semaphore_signal(
        barrier, inc=1, device_id=(plane(0, lax.rem(x + d, side), y), e_me), device_id_type=MESH))
    each(1, side, lambda d: pl.semaphore_signal(
        barrier, inc=1, device_id=(plane(0, x, lax.rem(y + d, side)), e_me), device_id_type=MESH))
    each(1, ep, lambda d: pl.semaphore_signal(
        barrier, inc=1, device_id=(s_me, other_ep(d)), device_id_type=MESH))

    load_queries = pltpu.make_async_copy(q, qraw, own_sem.at[chunks + 5])
    load_queries.start()

    def load_cache(i):
        return pltpu.make_async_copy(cache.at[i], kbuf.at[i], k_sem.at[i])

    slot = core * half + z
    values_here = pl.ds(pl.multiple_of(z * vdim, vdim), vdim)
    own_weights = [
        pltpu.make_async_copy(upv.at[0], upg.at[core, :, values_here], own_sem.at[chunks]),
        pltpu.make_async_copy(outp.at[0, :, pl.ds(pl.multiple_of(e_me * cols, cols), cols)], opr.at[slot], own_sem.at[chunks + 1]),
        pltpu.make_async_copy(down.at[0, :, pl.ds(pl.multiple_of(e_me * cols, cols), cols)], edr.at[e_me], own_sem.at[chunks + 2]),
        pltpu.make_async_copy(gate.at[0], gu.at[:, pl.ds(0, units)], own_sem.at[chunks + 3]),
        pltpu.make_async_copy(upw.at[0], gu.at[:, pl.ds(units, units)], own_sem.at[chunks + 4]),
    ]
    each(0, batch, lambda i: load_cache(i).start())
    for copy in own_weights:
        copy.start()
    res32[...] = res[...].astype(F32)
    gain32[...] = gain[...].astype(F32)
    resg[e_me] = res32[e_me]


    def pack(c):
        a, b = axes(lax.rem(c, 2))
        rows = [qraw[c * PAIR + j].astype(F32) for j in range(PAIR)]
        row = jnp.concatenate([r[:, :lat_dim] for r in rows] + [r[:, lat_dim:] for r in rows], axis=1)
        qg[c, a, b] = row.astype(BF16)

    load_queries.wait()
    each(0, chunks, pack)
    pl.semaphore_wait(barrier, 2 * (side - 1) + ep - 1)

    def gather_first(c):
        parity = lax.rem(c, 2)
        a, b = axes(parity)
        for d in range(1, side):
            send(qg.at[c, a, b], qg.at[c, a, b], a1_s.at[c], a1_r.at[c],
                 plane(parity, lax.rem(a + d, side), b), e_me)

    each(0, chunks, gather_first)
    left.append(lambda: each(0, chunks, lambda c: drain(qg.at[c, pl.ds(0, side - 1), 0], a1_s.at[c])))

    def spread_values(d):
        send(upv.at[0], upg.at[core, :, values_here], w_s.at[0], w_r.at[0], s_me, lax.rem(z + d, half) * 2 + core)

    def forward_values():
        own_weights[0].wait()
        drain(upg.at[0, :, pl.ds(0, (half - 1) * vdim)], w_r.at[0])
        send(upg.at[core], upg.at[core], c_s.at[2], c_r.at[2], s_me, sibling)

    def spread(d):
        e = other_ep(d)
        here = pl.ds(pl.multiple_of(e * cols, cols), cols)
        send(outp.at[0, :, here], opr.at[slot], w_s.at[1], w_r.at[1], s_me, e)
        send(res32.at[e], resg.at[e_me], w_s.at[3], w_r.at[3], s_me, e)

    def spread_down(hop, flip):
        e = lax.rem(z + hop, half) * 2 + lax.rem(core + flip, 2)
        here = pl.ds(pl.multiple_of(e * cols, cols), cols)
        send(down.at[0, :, here], edr.at[e_me], w_s.at[2], w_r.at[2], s_me, e)

    far = half // 2
    each(1, half, spread_values)
    each(1, ep, spread)
    spread_down(0, 1)
    for hop in range(1, half):
        if hop != far:
            spread_down(hop, 0)
            spread_down(hop, 1)

    left.append(lambda: drain(upg.at[0, :, pl.ds(0, (half - 1) * vdim)], w_s.at[0]))
    left.append(lambda: drain(opr.at[pl.ds(0, ep - 1)], w_s.at[1]))
    left.append(lambda: drain(resg.at[pl.ds(0, ep - 1)], w_s.at[3]))

    def gather_second(c):
        parity = lax.rem(c, 2)
        a, b = axes(parity)
        drain(qg.at[c, pl.ds(0, side - 1), 0], a1_r.at[c])
        for d in (1, side - 1):
            send(qg.at[c, :, b], qg.at[c, :, b], a2_s.at[c], a2_r.at[c],
                 plane(parity, a, lax.rem(b + d, side)), e_me)

    def gather_third(c):
        parity = lax.rem(c, 2)
        a, b = axes(parity)
        drain(qg.at[c, pl.ds(0, 2)], a2_r.at[c])
        for d, first in ((1, 0), (side - 1, side // 2)):
            to, came = lax.rem(b + d, side), lax.rem(b + side - d, side)
            part = qg.at[c, pl.ds(first, side // 2), came]
            send(part, part, a3_s.at[c], a3_r.at[c], plane(parity, a, to), e_me)

    def diagonal(rows, first):
        lane = lax.broadcasted_iota(jnp.int32, (rows, heads), 1)
        return lane == first + lax.broadcasted_iota(jnp.int32, (rows, heads), 0)

    eye = diagonal(heads, 0)

    def to_column(row, mask):
        return jnp.sum(jnp.where(mask, row, 0.0), axis=1, keepdims=True)

    position = s_me * span + lax.broadcasted_iota(jnp.int32, (1, span), 1)

    def attend(c):
        drain(qg.at[c, 0], a3_r.at[c])
        for j in range(PAIR):
            load_cache(c * PAIR + j).wait()
        packed = qg[c].astype(F32).reshape(heads, -1)
        split = PAIR * lat_dim
        rotary = (packed.shape[1] - split) // PAIR
        scores = [jnp.dot(
            jnp.concatenate([packed[:, j * lat_dim:(j + 1) * lat_dim],
                             packed[:, split + j * rotary:split + (j + 1) * rotary]], axis=1).astype(BF16),
            kbuf[c * PAIR + j], preferred_element_type=F32) for j in range(PAIR)]
        for j in range(PAIR):
            masked = jnp.where(position < lens[c * PAIR + j], scores[j], masked_score)
            top = jnp.max(masked, axis=1, keepdims=True)
            prob = jnp.exp2((masked - top) * (scale * math.log2(math.e)))
            total = jnp.sum(prob, axis=1, keepdims=True)
            mean = lax.dot_general(
                prob.astype(BF16), kbuf[c * PAIR + j, :lat_dim], (((1,), (1,)), ((), ())),
                preferred_element_type=F32) / total
            lat[c, :, j] = mean.reshape(side, side * group, lat_dim).astype(BF16)
            level = top * scale + jnp.log(total)
            st1_own[c, j:j + 1] = jnp.sum(jnp.where(eye, level, 0.0), axis=0, keepdims=True)
        parity = lax.rem(c, 2)
        a, b = axes(parity)
        for d in range(1, side):
            to = lax.rem(a + d, side)
            send(st1_own.at[c], st1.at[c, d - 1], st1_s.at[c], st1_r.at[c], plane(parity, to, b), e_me)
            send(lat.at[c, to], r1.at[c, d - 1], r1_s.at[c], r1_r.at[c], plane(parity, to, b), e_me)

    def merge(own_level, levels):
        top = jnp.maximum(own_level, jnp.max(levels, axis=0))
        weights = [jnp.exp(own_level - top)] + [jnp.exp(levels[d] - top) for d in range(side - 1)]
        den = sum(weights)
        return top + jnp.log(den), [w / den for w in weights]

    def sum_first(c):
        parity = lax.rem(c, 2)
        a, b = axes(parity)
        drain(st1.at[c], st1_r.at[c])
        level, weights = merge(st1_own[c], st1[c])
        st2_own[c] = level
        mask = diagonal(side * group, a * side * group)
        drain(r1.at[c], r1_r.at[c])
        for j in range(PAIR):
            total = lat[c, a, j].astype(F32) * to_column(weights[0][j:j + 1], mask)
            for d in range(side - 1):
                total += r1[c, d, j].astype(F32) * to_column(weights[d + 1][j:j + 1], mask)
            r2_own[c, :, j] = total.reshape(side, group, lat_dim).astype(BF16)
        for d in range(1, side):
            to = lax.rem(b + d, side)
            send(st2_own.at[c], st2.at[c, d - 1], st2_s.at[c], st2_r.at[c], plane(parity, a, to), e_me)
            send(r2_own.at[c, to], r2.at[c, d - 1], r2_s.at[c], r2_r.at[c], plane(parity, a, to), e_me)

    def sum_second(c):
        a, b = axes(lax.rem(c, 2))
        drain(st2.at[c], st2_r.at[c])
        _, weights = merge(st2_own[c], st2[c])
        mask = diagonal(group, (a * side + b) * group)
        drain(r2.at[c], r2_r.at[c])
        for j in range(PAIR):
            total = r2_own[c, b, j].astype(F32) * to_column(weights[0][j:j + 1], mask)
            for d in range(side - 1):
                total += r2[c, d, j].astype(F32) * to_column(weights[d + 1][j:j + 1], mask)
            latent[c * PAIR + j] = total

    window = 4
    each(0, min(window, chunks), gather_second)
    ahead = 2
    lag = 2

    def share_values(part):
        rows = batch // 2
        latents = latent[pl.ds(part * rows, rows)].reshape(rows * group, lat_dim).astype(BF16)
        values = jnp.concatenate([jnp.dot(latents, upg[k], preferred_element_type=F32) for k in range(2)], axis=1)
        row = lax.broadcasted_iota(jnp.int32, values.shape, 0)
        block = lax.div(lax.broadcasted_iota(jnp.int32, values.shape, 1), vdim)
        values = jnp.where(lax.rem(row, group) == lax.rem(block, half) * 2 + lax.div(block, half), values, 0.0)
        hv[e_me, part] = jnp.sum(values.reshape(rows, group, group * vdim), axis=1).astype(BF16)
        each(1, ep, lambda d: send(
            hv.at[e_me, part], hv.at[e_me, part], h_s.at[part], h_r.at[part], s_me, other_ep(d)))

    def first_values():
        drain(upg.at[0], c_r.at[2])
        share_values(0)

    def stage(i):
        pl.when(i == chunks // 2)(forward_values)

        def at(step, after):
            c = i - after
            pl.when(jnp.logical_and(c >= 0, c < chunks))(lambda: step(c))

        at(gather_third, 0)
        at(gather_second, -window)
        at(attend, ahead)
        at(sum_first, ahead + lag)
        at(sum_second, ahead + 2 * lag)
        pl.when(i == chunks // 2 - 1 + ahead + 2 * lag)(first_values)

    each(0, chunks + ahead + 2 * lag, stage)

    def sent(c):
        drain(qg.at[c, pl.ds(0, 2)], a2_s.at[c])
        drain(qg.at[c, 0], a3_s.at[c])
        drain(st1.at[c], st1_s.at[c])
        drain(st2.at[c], st2_s.at[c])
        drain(r1.at[c], r1_s.at[c])
        drain(r2.at[c], r2_s.at[c])

    left.append(lambda: each(0, chunks, sent))
    left.append(lambda: drain(upg.at[0], c_s.at[2]))

    share_values(1)
    own_weights[1].wait()
    drain(opr.at[pl.ds(0, ep - 1)], w_r.at[1])
    for part in range(2):
        drain(hv.at[pl.ds(0, ep - 1), part], h_r.at[part])
        left.append(lambda part=part: drain(hv.at[pl.ds(0, ep - 1), part], h_s.at[part]))
    attended = jnp.dot(
        hv[...].astype(F32).reshape(rows_all, group * vdim).astype(BF16), opr[...].reshape(ep * vdim, cols), preferred_element_type=F32)
    r5_own[...] = attended.reshape(seq, ep, cols).astype(BF16)
    each(1, seq, lambda d: send(
        r5_own.at[other_seq(d)], r5.at[d - 1], x_s.at[1], x_r.at[1], other_seq(d), e_me))
    left.append(lambda: drain(r5, x_s.at[1]))

    drain(resg.at[pl.ds(0, ep - 1)], w_r.at[3])
    residual = resg[...].reshape(ep, cols)
    lane = lax.broadcasted_iota(jnp.int32, (ep, EXTRA), 1)
    sub = lax.broadcasted_iota(jnp.int32, (ep, EXTRA), 0)
    expert = lax.div(lane - WEIGHT_LANE, 3)
    part = lax.rem(lane - WEIGHT_LANE, 3)
    weight = jnp.zeros((ep, EXTRA), F32)
    for k in range(routes.shape[1]):
        weight += jnp.where(expert == routes[0, k], route_w[0, k], 0.0)
    w_high, w_mid, w_low = three_parts(weight)
    weight = jnp.where(part == 0, w_high, jnp.where(part == 1, w_mid, w_low))
    weight = jnp.where(jnp.logical_and(sub == e_me, lane >= WEIGHT_LANE), weight, 0.0)

    drain(r5, x_r.at[1])
    hidden = r5_own[s_me].astype(F32)
    for d in range(seq - 1):
        hidden += r5[d].astype(F32)
    hidden = (hidden + residual).astype(BF16).astype(F32)
    hid[...] = hidden
    s_high, s_mid, s_low = three_parts(jnp.sum(hidden * hidden, axis=1, keepdims=True))
    squares = jnp.where(lane == 0, s_high, jnp.where(lane == 1, s_mid, jnp.where(lane == 2, s_low, 0.0)))
    per = cols // LANES
    gain_row = jnp.concatenate([gain32[pl.ds(e_me * per + k, 1), :] for k in range(per)], axis=1)
    row = jnp.concatenate([hidden * gain_row, squares + weight], axis=1).astype(BF16)

    def place(p, first, second, third):
        px, py, pz = ((first, second, third), (third, first, second), (second, third, first))[p]
        return px * side + py, pz * 2 + core

    here = ((x, y, z), (y, z, x), (z, x, y))
    for p in range(3):
        first, second, third = here[p]
        mine = first * side + second
        rows_p[p][third, mine] = row[:, cuts[p]:cuts[p + 1]]

        def to_plane(i, p=p, first=first, second=second, third=third, mine=mine):
            s, e = place(p, lax.rem(first + lax.div(i, side), side), lax.rem(second + lax.rem(i, side), side), third)
            send(rows_p[p].at[third, mine], rows_p[p].at[third, mine], p_s.at[p], p_r.at[p], s, e)

        each(1, seq, to_plane)
    for p in range(3):
        first, second, third = here[p]
        drain(rows_p[p].at[0, pl.ds(0, seq - 1)], p_r.at[p])
        for d in range(1, side):
            s, e = place(p, first, second, lax.rem(third + d, side))
            send(rows_p[p].at[third], rows_p[p].at[third], p_s.at[3 + p], p_r.at[3 + p], s, e)
        send(rows_p[p].at[third], rows_o[p].at[third], c_s.at[3 + p], c_r.at[3 + p], s_me, sibling)
    spread_down(far, 0)
    spread_down(far, 1)
    left.append(lambda: drain(edr.at[pl.ds(0, ep - 1)], w_s.at[2]))
    for p in range(3):
        third = here[p][2]
        drain(rows_p[p].at[pl.ds(0, side - 1)], p_r.at[3 + p])
        for d in range(1, side):
            at_d = lax.rem(third + d, side)
            send(rows_p[p].at[at_d], rows_o[p].at[at_d], c_s.at[3 + p], c_r.at[3 + p], s_me, sibling)

    def sent_rows():
        for p in range(3):
            drain(rows_p[p].at[0, pl.ds(0, seq - 1)], p_s.at[p])
            drain(rows_p[p].at[pl.ds(0, side - 1)], p_s.at[3 + p])
            drain(rows_o[p], c_s.at[3 + p])

    left.append(sent_rows)

    own_weights[3].wait()
    own_weights[4].wait()
    gated = jnp.zeros((rows_all, 2 * units), F32)
    extra = jnp.zeros((rows_all, EXTRA), F32)
    for other in range(2):
        if other:
            for p in range(3):
                drain(rows_o[p], c_r.at[3 + p])
        bufs = (rows_p, rows_o)[other]
        for k in range(side):
            parts = []
            for p in range(3):
                at_p = [((k, i * side + j), (i, j * side + k), (j, k * side + i))[p]
                        for i in range(side) for j in range(side)]
                parts.append(jnp.concatenate([bufs[p][at].astype(F32) for at in at_p], axis=0))
            rows = jnp.concatenate(parts, axis=1)
            e = 2 * k + core + other * (1 - 2 * core)
            span_e = pl.ds(pl.multiple_of(e * cols, cols), cols)
            gated += jnp.dot(rows[:, :cols].astype(BF16), gu[span_e, :], preferred_element_type=F32)
            extra += rows[:, cols:]

    lane = lax.broadcasted_iota(jnp.int32, extra.shape, 1)
    mine = WEIGHT_LANE + 3 * s_me
    squares = jnp.sum(jnp.where(lane < 3, extra, 0.0), axis=1, keepdims=True)
    weight = jnp.sum(jnp.where(jnp.logical_and(lane >= mine, lane < mine + 3), extra, 0.0), axis=1, keepdims=True)
    rms = lax.rsqrt(squares / width + 1e-6)
    gated = gated * rms
    gate_pre, up_pre = gated[:, :units], gated[:, units:]
    act[e_me] = (gate_pre / (1.0 + jnp.exp(-gate_pre)) * up_pre).astype(BF16)
    each(1, ep, lambda d: send(act.at[e_me], act.at[e_me], x_s.at[3], x_r.at[3], s_me, other_ep(d)))
    left.append(lambda: drain(act.at[pl.ds(0, ep - 1)], x_s.at[3]))

    own_weights[2].wait()
    drain(edr.at[pl.ds(0, ep - 1)], w_r.at[2])
    drain(act.at[pl.ds(0, ep - 1)], x_r.at[3])
    acts = jnp.concatenate([act[e] for e in range(ep)], axis=1)
    result = jnp.dot(acts, edr[...].reshape(ep * units, cols), preferred_element_type=F32) * weight
    r8_own[...] = result.reshape(seq, ep, cols).astype(BF16)
    each(1, seq, lambda d: send(
        r8_own.at[other_seq(d)], r8.at[d - 1], x_s.at[4], x_r.at[4], other_seq(d), e_me))
    left.append(lambda: drain(r8, x_s.at[4]))

    drain(r8, x_r.at[4])
    mixed = r8_own[s_me].astype(F32)
    for d in range(seq - 1):
        mixed += r8[d].astype(F32)
    mixed = mixed + hid[...]
    mix_own[...] = mixed.reshape(ep, 1, cols)
    mix_got[e_me] = mix_own[e_me]
    each(1, ep, lambda d: send(
        mix_own.at[other_ep(d)], mix_got.at[e_me], x_s.at[5], x_r.at[5], s_me, other_ep(d)))
    left.append(lambda: drain(mix_got.at[pl.ds(0, ep - 1)], x_s.at[5]))
    drain(mix_got.at[pl.ds(0, ep - 1)], x_r.at[5])
    out[...] = mix_got[...]

    finish()


def shards(
    seq, ep, latent_cache, queries, lengths, up_value, out_proj, residual, norm_gain,
    routes, route_weight, expert_gate, expert_up, expert_down,
):
    side = math.isqrt(seq)
    batch, span, kdim = latent_cache.shape
    group = queries.shape[1]
    heads = group * seq
    lat_dim, vdim = up_value.shape[1:]
    width = residual.shape[1]
    cols = width // ep
    units = expert_gate.shape[2]
    chunks = batch // PAIR
    rows_all = seq * ep
    dma = pltpu.SemaphoreType.DMA
    vmem = pltpu.VMEM
    cuts = row_cuts(cols)
    row_parts = [vmem((side, seq, ep, cuts[p + 1] - cuts[p]), BF16) for p in range(3)]
    scratch = [
        vmem((batch, kdim, span), BF16),
        vmem((batch, group, kdim), BF16),
        vmem((chunks, side, side, group, PAIR * kdim), BF16),
        vmem((chunks, PAIR, heads), F32),
        vmem((chunks, side - 1, PAIR, heads), F32),
        vmem((chunks, side, PAIR, side * group, lat_dim), BF16),
        vmem((chunks, side - 1, PAIR, side * group, lat_dim), BF16),
        vmem((chunks, PAIR, heads), F32),
        vmem((chunks, side - 1, PAIR, heads), F32),
        vmem((chunks, side, PAIR, group, lat_dim), BF16),
        vmem((chunks, side - 1, PAIR, group, lat_dim), BF16),
        vmem((batch, group, lat_dim), F32),
        vmem((ep, 1, cols), F32),
        vmem((width // LANES, LANES), F32),
        vmem((2, lat_dim, ep // 2 * vdim), BF16),
        vmem((ep, vdim, cols), BF16),
        vmem((ep, units, cols), BF16),
        vmem((width, 2 * units), BF16),
        vmem((ep, 2, batch // 2, group * vdim), BF16),
        vmem((seq, ep, cols), BF16),
        vmem((seq - 1, ep, cols), BF16),
        vmem((ep, 1, cols), F32),
        vmem((ep, cols), F32),
        *row_parts, *row_parts,
        vmem((ep, rows_all, units), BF16),
        vmem((seq, ep, cols), BF16),
        vmem((seq - 1, ep, cols), BF16),
        vmem((ep, 1, cols), F32),
        vmem((ep, 1, cols), F32),
        dma((batch,)),
        dma((chunks + 6,)),
    ]
    scratch += [dma((chunks,)) for _ in range(14)]
    scratch += [dma((4,)), dma((4,)), dma((6,)), dma((6,)), dma((6,)), dma((6,)), dma((6,)), dma((6,)), dma((2,)), dma((2,))]
    smem = pl.BlockSpec(memory_space=pltpu.SMEM)
    whole = pl.BlockSpec(memory_space=pltpu.VMEM)
    anywhere = pl.BlockSpec(memory_space=pl.ANY)
    mixed = pl.pallas_call(
        functools.partial(decode_kernel, side, ep, 192.0 ** (-0.5), width),
        out_shape=jax.ShapeDtypeStruct((ep, 1, cols), F32),
        in_specs=[smem, smem, smem] + [anywhere] * 4 + [whole, whole] + [anywhere] * 3,
        out_specs=whole,
        scratch_shapes=scratch,
        compiler_params=pltpu.CompilerParams(
            collective_id=0, has_side_effects=True, vmem_limit_bytes=58 * 1024 * 1024),
        name="decode",
    )(
        lengths, routes, route_weight, jnp.swapaxes(latent_cache, 1, 2), queries, up_value, out_proj,
        residual.reshape(ep, 1, cols), norm_gain.reshape(width // LANES, LANES),
        expert_gate, expert_up, expert_down,
    )
    return mixed.reshape(1, width).astype(BF16)


def solution(mesh):
    placed = (
        P("ep", "seq", None),
        P("ep", "seq", None),
        P("ep"),
        P(("seq", "ep"), None, None),
        P(("seq", "ep"), None, None),
        P(("seq", "ep"), None),
        P(),
        P(("seq", "ep"), None),
        P(("seq", "ep"), None),
        P("seq", None, "ep"),
        P("seq", None, "ep"),
        P("seq", "ep", None),
    )
    return jax.shard_map(
        functools.partial(shards, mesh.shape["seq"], mesh.shape["ep"]),
        mesh=mesh, in_specs=placed, out_specs=P(("seq", "ep"), None), check_vma=False,
    )
```

```python
import functools
import math

import jax
import jax.numpy as jnp
from jax import lax
from jax.experimental import pallas as pl
from jax.experimental.pallas import tpu as pltpu
from jax.sharding import PartitionSpec as P

MESH = pl.DeviceIdType.MESH
F32 = jnp.float32
BF16 = jnp.bfloat16
masked_score = -1e30
PAIR = 2
LANES = 128
EXTRA = LANES
WEIGHT_LANE = 16


def three_parts(value):
    high = value.astype(BF16).astype(F32)
    rest = value - high
    middle = rest.astype(BF16).astype(F32)
    return high, middle, (rest - middle).astype(BF16).astype(F32)


def row_cuts(cols):
    tiles = (cols + EXTRA) // LANES
    return [LANES * (tiles * p // 3) for p in range(3)] + [cols + EXTRA]


def drain(ref, sem):
    pltpu.make_async_copy(ref, ref, sem).wait()


def decode_kernel(
    side, ep, scale, width,
    lens, routes, route_w, cache, q, upv, outp, res, gain, gate, upw, down,
    out,
    kbuf, qraw, qg, st1_own, st1, lat, r1, st2_own, st2, r2_own, r2, latent, res32, gain32,
    upg, opr, edr, gu, hv, r5_own, r5, resg, hid, rows_a, rows_b, rows_c, rows_oa, rows_ob, rows_oc, act, r8_own, r8, mix_own, mix_got,
    k_sem, own_sem, a1_s, a1_r, a2_s, a2_r, a3_s, a3_r, st1_s, st1_r, st2_s, st2_r, r1_s, r1_r, r2_s, r2_r,
    w_s, w_r, x_s, x_r, p_s, p_r, c_s, c_r, h_s, h_r,
):
    seq = side * side
    batch, _, span = kbuf.shape
    chunks = batch // PAIR
    group, lat_dim = latent.shape[1:]
    heads = group * seq
    vdim = upv.shape[2]
    cols = opr.shape[2]
    units = gate.shape[2]
    half = ep // 2
    rows_all = seq * ep

    s_me = lax.axis_index("seq")
    e_me = lax.axis_index("ep")
    x, y = lax.div(s_me, side), lax.rem(s_me, side)
    z, core = lax.div(e_me, 2), lax.rem(e_me, 2)
    sibling = e_me + 1 - 2 * core

    def axes(parity):
        return x + parity * (y - x), y + parity * (x - y)

    def plane(parity, a, b):
        return (a * side + b) + parity * ((b * side + a) - (a * side + b))

    def send(src, dst, send_sem, recv_sem, s, e):
        pltpu.make_async_remote_copy(
            src_ref=src, dst_ref=dst, send_sem=send_sem, recv_sem=recv_sem,
            device_id=(s, e), device_id_type=MESH,
        ).start()

    def each(lo, hi, body):
        lax.fori_loop(lo, hi, lambda i, c: (body(i), c)[1], 0)

    def unrolled(lo, hi, body):
        for i in range(lo, hi):
            body(i)

    def other_seq(d):
        return lax.rem(s_me + d, seq)

    def other_ep(d):
        return lax.rem(e_me + d, ep)

    cuts = row_cuts(cols)
    rows_p, rows_o = (rows_a, rows_b, rows_c), (rows_oa, rows_ob, rows_oc)
    left = []

    def finish():
        for wait in left:
            wait()

    barrier = pltpu.get_barrier_semaphore()
    unrolled(1, side, lambda d: pl.semaphore_signal(
        barrier, inc=1, device_id=(plane(0, lax.rem(x + d, side), y), e_me), device_id_type=MESH))
    unrolled(1, side, lambda d: pl.semaphore_signal(
        barrier, inc=1, device_id=(plane(0, x, lax.rem(y + d, side)), e_me), device_id_type=MESH))
    unrolled(1, ep, lambda d: pl.semaphore_signal(
        barrier, inc=1, device_id=(s_me, other_ep(d)), device_id_type=MESH))

    load_queries = pltpu.make_async_copy(q, qraw, own_sem.at[chunks + 5])
    load_queries.start()

    def load_cache(i):
        return pltpu.make_async_copy(cache.at[i], kbuf.at[i], k_sem.at[i])

    slot = core * half + z
    values_here = pl.ds(pl.multiple_of(z * vdim, vdim), vdim)
    own_weights = [
        pltpu.make_async_copy(upv.at[0], upg.at[core, :, values_here], own_sem.at[chunks]),
        pltpu.make_async_copy(outp.at[0, :, pl.ds(pl.multiple_of(e_me * cols, cols), cols)], opr.at[slot], own_sem.at[chunks + 1]),
        pltpu.make_async_copy(down.at[0, :, pl.ds(pl.multiple_of(e_me * cols, cols), cols)], edr.at[e_me], own_sem.at[chunks + 2]),
        pltpu.make_async_copy(gate.at[0], gu.at[:, pl.ds(0, units)], own_sem.at[chunks + 3]),
        pltpu.make_async_copy(upw.at[0], gu.at[:, pl.ds(units, units)], own_sem.at[chunks + 4]),
    ]
    each(0, batch, lambda i: load_cache(i).start())
    for copy in own_weights:
        copy.start()
    res32[...] = res[...].astype(F32)
    gain32[...] = gain[...].astype(F32)
    resg[e_me] = res32[e_me]


    def pack(c):
        a, b = axes(lax.rem(c, 2))
        rows = [qraw[c * PAIR + j].astype(F32) for j in range(PAIR)]
        row = jnp.concatenate([r[:, :lat_dim] for r in rows] + [r[:, lat_dim:] for r in rows], axis=1)
        qg[c, a, b] = row.astype(BF16)

    load_queries.wait()
    each(0, chunks, pack)
    pl.semaphore_wait(barrier, 2 * (side - 1) + ep - 1)

    def gather_first(c):
        parity = lax.rem(c, 2)
        a, b = axes(parity)
        for d in range(1, side):
            send(qg.at[c, a, b], qg.at[c, a, b], a1_s.at[c], a1_r.at[c],
                 plane(parity, lax.rem(a + d, side), b), e_me)

    each(0, chunks, gather_first)
    left.append(lambda: each(0, chunks, lambda c: drain(qg.at[c, pl.ds(0, side - 1), 0], a1_s.at[c])))

    def spread_values(d):
        send(upv.at[0], upg.at[core, :, values_here], w_s.at[0], w_r.at[0], s_me, lax.rem(z + d, half) * 2 + core)

    def forward_values():
        own_weights[0].wait()
        drain(upg.at[0, :, pl.ds(0, (half - 1) * vdim)], w_r.at[0])
        send(upg.at[core], upg.at[core], c_s.at[2], c_r.at[2], s_me, sibling)

    def spread(d):
        e = other_ep(d)
        here = pl.ds(pl.multiple_of(e * cols, cols), cols)
        send(outp.at[0, :, here], opr.at[slot], w_s.at[1], w_r.at[1], s_me, e)
        send(res32.at[e], resg.at[e_me], w_s.at[3], w_r.at[3], s_me, e)

    def spread_down(hop, flip):
        e = lax.rem(z + hop, half) * 2 + lax.rem(core + flip, 2)
        here = pl.ds(pl.multiple_of(e * cols, cols), cols)
        send(down.at[0, :, here], edr.at[e_me], w_s.at[2], w_r.at[2], s_me, e)

    far = half // 2
    unrolled(1, half, spread_values)
    unrolled(1, ep, spread)
    spread_down(0, 1)
    for hop in range(1, half):
        if hop != far:
            spread_down(hop, 0)
            spread_down(hop, 1)

    left.append(lambda: drain(upg.at[0, :, pl.ds(0, (half - 1) * vdim)], w_s.at[0]))
    left.append(lambda: drain(opr.at[pl.ds(0, ep - 1)], w_s.at[1]))
    left.append(lambda: drain(resg.at[pl.ds(0, ep - 1)], w_s.at[3]))

    def gather_second(c):
        parity = lax.rem(c, 2)
        a, b = axes(parity)
        drain(qg.at[c, pl.ds(0, side - 1), 0], a1_r.at[c])
        for d in (1, side - 1):
            send(qg.at[c, :, b], qg.at[c, :, b], a2_s.at[c], a2_r.at[c],
                 plane(parity, a, lax.rem(b + d, side)), e_me)

    def gather_third(c):
        parity = lax.rem(c, 2)
        a, b = axes(parity)
        drain(qg.at[c, pl.ds(0, 2)], a2_r.at[c])
        for d, first in ((1, 0), (side - 1, side // 2)):
            to, came = lax.rem(b + d, side), lax.rem(b + side - d, side)
            part = qg.at[c, pl.ds(first, side // 2), came]
            send(part, part, a3_s.at[c], a3_r.at[c], plane(parity, a, to), e_me)

    def diagonal(rows, first):
        lane = lax.broadcasted_iota(jnp.int32, (rows, heads), 1)
        return lane == first + lax.broadcasted_iota(jnp.int32, (rows, heads), 0)

    eye = diagonal(heads, 0)

    def to_column(row, mask):
        return jnp.sum(jnp.where(mask, row, 0.0), axis=1, keepdims=True)

    position = s_me * span + lax.broadcasted_iota(jnp.int32, (1, span), 1)

    def attend(c):
        drain(qg.at[c, 0], a3_r.at[c])
        for j in range(PAIR):
            load_cache(c * PAIR + j).wait()
        packed = qg[c].astype(F32).reshape(heads, -1)
        split = PAIR * lat_dim
        rotary = (packed.shape[1] - split) // PAIR
        scores = [jnp.dot(
            jnp.concatenate([packed[:, j * lat_dim:(j + 1) * lat_dim],
                             packed[:, split + j * rotary:split + (j + 1) * rotary]], axis=1).astype(BF16),
            kbuf[c * PAIR + j], preferred_element_type=F32) for j in range(PAIR)]
        for j in range(PAIR):
            masked = jnp.where(position < lens[c * PAIR + j], scores[j], masked_score)
            top = jnp.max(masked, axis=1, keepdims=True)
            prob = jnp.exp2((masked - top) * (scale * math.log2(math.e)))
            total = jnp.sum(prob, axis=1, keepdims=True)
            mean = lax.dot_general(
                prob.astype(BF16), kbuf[c * PAIR + j, :lat_dim], (((1,), (1,)), ((), ())),
                preferred_element_type=F32) / total
            lat[c, :, j] = mean.reshape(side, side * group, lat_dim).astype(BF16)
            level = top * scale + jnp.log(total)
            st1_own[c, j:j + 1] = jnp.sum(jnp.where(eye, level, 0.0), axis=0, keepdims=True)
        parity = lax.rem(c, 2)
        a, b = axes(parity)
        for d in range(1, side):
            to = lax.rem(a + d, side)
            send(st1_own.at[c], st1.at[c, d - 1], st1_s.at[c], st1_r.at[c], plane(parity, to, b), e_me)
            send(lat.at[c, to], r1.at[c, d - 1], r1_s.at[c], r1_r.at[c], plane(parity, to, b), e_me)

    def merge(own_level, levels):
        top = jnp.maximum(own_level, jnp.max(levels, axis=0))
        weights = [jnp.exp(own_level - top)] + [jnp.exp(levels[d] - top) for d in range(side - 1)]
        den = sum(weights)
        return top + jnp.log(den), [w / den for w in weights]

    def sum_first(c):
        parity = lax.rem(c, 2)
        a, b = axes(parity)
        drain(st1.at[c], st1_r.at[c])
        level, weights = merge(st1_own[c], st1[c])
        st2_own[c] = level
        mask = diagonal(side * group, a * side * group)
        drain(r1.at[c], r1_r.at[c])
        for j in range(PAIR):
            total = lat[c, a, j].astype(F32) * to_column(weights[0][j:j + 1], mask)
            for d in range(side - 1):
                total += r1[c, d, j].astype(F32) * to_column(weights[d + 1][j:j + 1], mask)
            r2_own[c, :, j] = total.reshape(side, group, lat_dim).astype(BF16)
        for d in range(1, side):
            to = lax.rem(b + d, side)
            send(st2_own.at[c], st2.at[c, d - 1], st2_s.at[c], st2_r.at[c], plane(parity, a, to), e_me)
            send(r2_own.at[c, to], r2.at[c, d - 1], r2_s.at[c], r2_r.at[c], plane(parity, a, to), e_me)

    def sum_second(c):
        a, b = axes(lax.rem(c, 2))
        drain(st2.at[c], st2_r.at[c])
        _, weights = merge(st2_own[c], st2[c])
        mask = diagonal(group, (a * side + b) * group)
        drain(r2.at[c], r2_r.at[c])
        for j in range(PAIR):
            total = r2_own[c, b, j].astype(F32) * to_column(weights[0][j:j + 1], mask)
            for d in range(side - 1):
                total += r2[c, d, j].astype(F32) * to_column(weights[d + 1][j:j + 1], mask)
            latent[c * PAIR + j] = total

    window = 4
    each(0, min(window, chunks), gather_second)
    ahead = 2
    lag = 2

    def share_values(part):
        rows = batch // 2
        latents = latent[pl.ds(part * rows, rows)].reshape(rows * group, lat_dim).astype(BF16)
        values = jnp.concatenate([jnp.dot(latents, upg[k], preferred_element_type=F32) for k in range(2)], axis=1)
        row = lax.broadcasted_iota(jnp.int32, values.shape, 0)
        block = lax.div(lax.broadcasted_iota(jnp.int32, values.shape, 1), vdim)
        values = jnp.where(lax.rem(row, group) == lax.rem(block, half) * 2 + lax.div(block, half), values, 0.0)
        hv[e_me, part] = jnp.sum(values.reshape(rows, group, group * vdim), axis=1).astype(BF16)
        unrolled(1, ep, lambda d: send(
            hv.at[e_me, part], hv.at[e_me, part], h_s.at[part], h_r.at[part], s_me, other_ep(d)))

    def first_values():
        drain(upg.at[0], c_r.at[2])
        share_values(0)

    def stage(i):
        pl.when(i == chunks // 2)(forward_values)

        def at(step, after):
            c = i - after
            pl.when(jnp.logical_and(c >= 0, c < chunks))(lambda: step(c))

        at(gather_third, 0)
        at(gather_second, -window)
        at(attend, ahead)
        at(sum_first, ahead + lag)
        at(sum_second, ahead + 2 * lag)
        pl.when(i == chunks // 2 - 1 + ahead + 2 * lag)(first_values)

    each(0, chunks + ahead + 2 * lag, stage)

    def sent(c):
        drain(qg.at[c, pl.ds(0, 2)], a2_s.at[c])
        drain(qg.at[c, 0], a3_s.at[c])
        drain(st1.at[c], st1_s.at[c])
        drain(st2.at[c], st2_s.at[c])
        drain(r1.at[c], r1_s.at[c])
        drain(r2.at[c], r2_s.at[c])

    left.append(lambda: each(0, chunks, sent))
    left.append(lambda: drain(upg.at[0], c_s.at[2]))

    share_values(1)
    own_weights[1].wait()
    drain(opr.at[pl.ds(0, ep - 1)], w_r.at[1])
    for part in range(2):
        drain(hv.at[pl.ds(0, ep - 1), part], h_r.at[part])
        left.append(lambda part=part: drain(hv.at[pl.ds(0, ep - 1), part], h_s.at[part]))
    attended = jnp.dot(
        hv[...].astype(F32).reshape(rows_all, group * vdim).astype(BF16), opr[...].reshape(ep * vdim, cols), preferred_element_type=F32)
    r5_own[...] = attended.reshape(seq, ep, cols).astype(BF16)
    unrolled(1, seq, lambda d: send(
        r5_own.at[other_seq(d)], r5.at[d - 1], x_s.at[1], x_r.at[1], other_seq(d), e_me))
    left.append(lambda: drain(r5, x_s.at[1]))

    drain(resg.at[pl.ds(0, ep - 1)], w_r.at[3])
    residual = resg[...].reshape(ep, cols)
    lane = lax.broadcasted_iota(jnp.int32, (ep, EXTRA), 1)
    sub = lax.broadcasted_iota(jnp.int32, (ep, EXTRA), 0)
    expert = lax.div(lane - WEIGHT_LANE, 3)
    part = lax.rem(lane - WEIGHT_LANE, 3)
    weight = jnp.zeros((ep, EXTRA), F32)
    for k in range(routes.shape[1]):
        weight += jnp.where(expert == routes[0, k], route_w[0, k], 0.0)
    w_high, w_mid, w_low = three_parts(weight)
    weight = jnp.where(part == 0, w_high, jnp.where(part == 1, w_mid, w_low))
    weight = jnp.where(jnp.logical_and(sub == e_me, lane >= WEIGHT_LANE), weight, 0.0)

    drain(r5, x_r.at[1])
    hidden = r5_own[s_me].astype(F32)
    for d in range(seq - 1):
        hidden += r5[d].astype(F32)
    hidden = (hidden + residual).astype(BF16).astype(F32)
    hid[...] = hidden
    s_high, s_mid, s_low = three_parts(jnp.sum(hidden * hidden, axis=1, keepdims=True))
    squares = jnp.where(lane == 0, s_high, jnp.where(lane == 1, s_mid, jnp.where(lane == 2, s_low, 0.0)))
    per = cols // LANES
    gain_row = jnp.concatenate([gain32[pl.ds(e_me * per + k, 1), :] for k in range(per)], axis=1)
    row = jnp.concatenate([hidden * gain_row, squares + weight], axis=1).astype(BF16)

    def place(p, first, second, third):
        px, py, pz = ((first, second, third), (third, first, second), (second, third, first))[p]
        return px * side + py, pz * 2 + core

    here = ((x, y, z), (y, z, x), (z, x, y))
    for p in range(3):
        first, second, third = here[p]
        mine = first * side + second
        rows_p[p][third, mine] = row[:, cuts[p]:cuts[p + 1]]

        def to_plane(i, p=p, first=first, second=second, third=third, mine=mine):
            s, e = place(p, lax.rem(first + i // side, side), lax.rem(second + i % side, side), third)
            send(rows_p[p].at[third, mine], rows_p[p].at[third, mine], p_s.at[p], p_r.at[p], s, e)

        unrolled(1, seq, to_plane)
    for p in range(3):
        first, second, third = here[p]
        drain(rows_p[p].at[0, pl.ds(0, seq - 1)], p_r.at[p])
        for d in range(1, side):
            s, e = place(p, first, second, lax.rem(third + d, side))
            send(rows_p[p].at[third], rows_p[p].at[third], p_s.at[3 + p], p_r.at[3 + p], s, e)
        send(rows_p[p].at[third], rows_o[p].at[third], c_s.at[3 + p], c_r.at[3 + p], s_me, sibling)
    spread_down(far, 0)
    spread_down(far, 1)
    left.append(lambda: drain(edr.at[pl.ds(0, ep - 1)], w_s.at[2]))
    for p in range(3):
        third = here[p][2]
        drain(rows_p[p].at[pl.ds(0, side - 1)], p_r.at[3 + p])
        for d in range(1, side):
            at_d = lax.rem(third + d, side)
            send(rows_p[p].at[at_d], rows_o[p].at[at_d], c_s.at[3 + p], c_r.at[3 + p], s_me, sibling)

    def sent_rows():
        for p in range(3):
            drain(rows_p[p].at[0, pl.ds(0, seq - 1)], p_s.at[p])
            drain(rows_p[p].at[pl.ds(0, side - 1)], p_s.at[3 + p])
            drain(rows_o[p], c_s.at[3 + p])

    left.append(sent_rows)

    own_weights[3].wait()
    own_weights[4].wait()
    gated = jnp.zeros((rows_all, 2 * units), F32)
    extra = jnp.zeros((rows_all, EXTRA), F32)
    for other in range(2):
        if other:
            for p in range(3):
                drain(rows_o[p], c_r.at[3 + p])
        bufs = (rows_p, rows_o)[other]
        for k in range(side):
            parts = []
            for p in range(3):
                at_p = [((k, i * side + j), (i, j * side + k), (j, k * side + i))[p]
                        for i in range(side) for j in range(side)]
                parts.append(jnp.concatenate([bufs[p][at].astype(F32) for at in at_p], axis=0))
            rows = jnp.concatenate(parts, axis=1)
            e = 2 * k + core + other * (1 - 2 * core)
            span_e = pl.ds(pl.multiple_of(e * cols, cols), cols)
            gated += jnp.dot(rows[:, :cols].astype(BF16), gu[span_e, :], preferred_element_type=F32)
            extra += rows[:, cols:]

    lane = lax.broadcasted_iota(jnp.int32, extra.shape, 1)
    mine = WEIGHT_LANE + 3 * s_me
    squares = jnp.sum(jnp.where(lane < 3, extra, 0.0), axis=1, keepdims=True)
    weight = jnp.sum(jnp.where(jnp.logical_and(lane >= mine, lane < mine + 3), extra, 0.0), axis=1, keepdims=True)
    rms = lax.rsqrt(squares / width + 1e-6)
    gated = gated * rms
    gate_pre, up_pre = gated[:, :units], gated[:, units:]
    act[e_me] = (gate_pre / (1.0 + jnp.exp(-gate_pre)) * up_pre).astype(BF16)
    unrolled(1, ep, lambda d: send(act.at[e_me], act.at[e_me], x_s.at[3], x_r.at[3], s_me, other_ep(d)))
    left.append(lambda: drain(act.at[pl.ds(0, ep - 1)], x_s.at[3]))

    own_weights[2].wait()
    drain(edr.at[pl.ds(0, ep - 1)], w_r.at[2])
    drain(act.at[pl.ds(0, ep - 1)], x_r.at[3])
    acts = jnp.concatenate([act[e] for e in range(ep)], axis=1)
    result = jnp.dot(acts, edr[...].reshape(ep * units, cols), preferred_element_type=F32) * weight
    r8_own[...] = result.reshape(seq, ep, cols).astype(BF16)
    unrolled(1, seq, lambda d: send(
        r8_own.at[other_seq(d)], r8.at[d - 1], x_s.at[4], x_r.at[4], other_seq(d), e_me))
    left.append(lambda: drain(r8, x_s.at[4]))

    drain(r8, x_r.at[4])
    mixed = r8_own[s_me].astype(F32)
    for d in range(seq - 1):
        mixed += r8[d].astype(F32)
    mixed = mixed + hid[...]
    mix_own[...] = mixed.reshape(ep, 1, cols)
    mix_got[e_me] = mix_own[e_me]
    unrolled(1, ep, lambda d: send(
        mix_own.at[other_ep(d)], mix_got.at[e_me], x_s.at[5], x_r.at[5], s_me, other_ep(d)))
    left.append(lambda: drain(mix_got.at[pl.ds(0, ep - 1)], x_s.at[5]))
    drain(mix_got.at[pl.ds(0, ep - 1)], x_r.at[5])
    out[...] = mix_got[...]

    finish()


def shards(
    seq, ep, latent_cache, queries, lengths, up_value, out_proj, residual, norm_gain,
    routes, route_weight, expert_gate, expert_up, expert_down,
):
    side = math.isqrt(seq)
    batch, span, kdim = latent_cache.shape
    group = queries.shape[1]
    heads = group * seq
    lat_dim, vdim = up_value.shape[1:]
    width = residual.shape[1]
    cols = width // ep
    units = expert_gate.shape[2]
    chunks = batch // PAIR
    rows_all = seq * ep
    dma = pltpu.SemaphoreType.DMA
    vmem = pltpu.VMEM
    cuts = row_cuts(cols)
    row_parts = [vmem((side, seq, ep, cuts[p + 1] - cuts[p]), BF16) for p in range(3)]
    scratch = [
        vmem((batch, kdim, span), BF16),
        vmem((batch, group, kdim), BF16),
        vmem((chunks, side, side, group, PAIR * kdim), BF16),
        vmem((chunks, PAIR, heads), F32),
        vmem((chunks, side - 1, PAIR, heads), F32),
        vmem((chunks, side, PAIR, side * group, lat_dim), BF16),
        vmem((chunks, side - 1, PAIR, side * group, lat_dim), BF16),
        vmem((chunks, PAIR, heads), F32),
        vmem((chunks, side - 1, PAIR, heads), F32),
        vmem((chunks, side, PAIR, group, lat_dim), BF16),
        vmem((chunks, side - 1, PAIR, group, lat_dim), BF16),
        vmem((batch, group, lat_dim), F32),
        vmem((ep, 1, cols), F32),
        vmem((width // LANES, LANES), F32),
        vmem((2, lat_dim, ep // 2 * vdim), BF16),
        vmem((ep, vdim, cols), BF16),
        vmem((ep, units, cols), BF16),
        vmem((width, 2 * units), BF16),
        vmem((ep, 2, batch // 2, group * vdim), BF16),
        vmem((seq, ep, cols), BF16),
        vmem((seq - 1, ep, cols), BF16),
        vmem((ep, 1, cols), F32),
        vmem((ep, cols), F32),
        *row_parts, *row_parts,
        vmem((ep, rows_all, units), BF16),
        vmem((seq, ep, cols), BF16),
        vmem((seq - 1, ep, cols), BF16),
        vmem((ep, 1, cols), F32),
        vmem((ep, 1, cols), F32),
        dma((batch,)),
        dma((chunks + 6,)),
    ]
    scratch += [dma((chunks,)) for _ in range(14)]
    scratch += [dma((4,)), dma((4,)), dma((6,)), dma((6,)), dma((6,)), dma((6,)), dma((6,)), dma((6,)), dma((2,)), dma((2,))]
    smem = pl.BlockSpec(memory_space=pltpu.SMEM)
    whole = pl.BlockSpec(memory_space=pltpu.VMEM)
    anywhere = pl.BlockSpec(memory_space=pl.ANY)
    mixed = pl.pallas_call(
        functools.partial(decode_kernel, side, ep, 192.0 ** (-0.5), width),
        out_shape=jax.ShapeDtypeStruct((ep, 1, cols), F32),
        in_specs=[smem, smem, smem] + [anywhere] * 4 + [whole, whole] + [anywhere] * 3,
        out_specs=whole,
        scratch_shapes=scratch,
        compiler_params=pltpu.CompilerParams(
            collective_id=0, has_side_effects=True, vmem_limit_bytes=58 * 1024 * 1024),
        name="decode",
    )(
        lengths, routes, route_weight, jnp.swapaxes(latent_cache, 1, 2), queries, up_value, out_proj,
        residual.reshape(ep, 1, cols), norm_gain.reshape(width // LANES, LANES),
        expert_gate, expert_up, expert_down,
    )
    return mixed.reshape(1, width).astype(BF16)


def solution(mesh):
    placed = (
        P("ep", "seq", None),
        P("ep", "seq", None),
        P("ep"),
        P(("seq", "ep"), None, None),
        P(("seq", "ep"), None, None),
        P(("seq", "ep"), None),
        P(),
        P(("seq", "ep"), None),
        P(("seq", "ep"), None),
        P("seq", None, "ep"),
        P("seq", None, "ep"),
        P("seq", "ep", None),
    )
    return jax.shard_map(
        functools.partial(shards, mesh.shape["seq"], mesh.shape["ep"]),
        mesh=mesh, in_specs=placed, out_specs=P(("seq", "ep"), None), check_vma=False,
    )
```
